32 devices in a mesh: hist: 8 (over y, x, core), second: 4 (over z).
Axes of the slice: x: 2, y: 2, z: 4, core: 2. Of those that a mesh axis runs over, the one named last changes fastest.
Arguments:
- history: bfloat16 [8192, 8192], P('hist', 'second'), may hold values from -0.0625 to 0.0625
- self_rows: bfloat16 [256, 8192], P(None, 'hist'), may hold values from -6 to 6
- edge_rows: bfloat16 [128, 8192], P(None, 'second'), may hold values from -6 to 6
- step_inv: float32 [128, 128], replicated, may hold values from -0.08 to 0.98, as said below
- coupling: float32 [128], replicated, may hold values from 0.1 to 1
- reach: int32 [3, 64], replicated, may hold values from 1 to 64, as said below
Outputs:
- green_last: bfloat16 [256, 8192], P(None, 'second')
The draws below stay inside these ranges and needn't reach their ends.
Inputs may be any that keep to these rules, and one draw needn't show every extreme that they name: `step_inv`: entries other than the diagonal lie within 0.08 of zero; diagonal entries between 0.5 and 0.9. reach[b, c] is at least c + 1 and at most min(64, c + 2 * b + 4).
All inputs are finite; a program needn't handle non-finite values.
Results may differ from the reference program's by a relative error of at most 0.014.
Values may be sent and summed in bfloat16 or wider, within the bound.
A program may use at most 64 MiB of HBM per device.

```python
import math
import jax
import jax.numpy as jnp
from jax import lax

TPB = 2
NBLK = 3
ROW_T = 128
ROWS = 256
P_SIZE = 64
KH = 8192
N_HIST = 8


def draw_step_inv(key, part):
    first_key, second_key = jax.random.split(jax.random.fold_in(key, 11))
    diagonal = jax.random.uniform(first_key, (ROW_T,), jnp.float32, 0.5, 0.9)
    spread = 0.25 / ROW_T ** 0.5
    others = jax.random.normal(second_key, (ROW_T, ROW_T), jnp.float32) * spread
    others = jnp.clip(others, -0.08, 0.08)
    others = others * (1.0 - jnp.eye(ROW_T, dtype=jnp.float32))
    return (others + jnp.diag(diagonal)).astype(jnp.float32)


def draw_reach(key, part):
    offsets = jax.random.randint(jax.random.fold_in(key, 23), (NBLK, P_SIZE), 0, 4)
    columns = jnp.arange(P_SIZE, dtype=jnp.int32)[None, :]
    sections = jnp.arange(NBLK, dtype=jnp.int32)[:, None]
    return jnp.minimum(columns + 1 + 2 * sections + offsets, P_SIZE).astype(jnp.int32)


def block_levels(rng, dims, cuts, smallest, largest):
    factor_of, own = 1.0, jax.random.fold_in(rng, 6)
    for position, shards_of in cuts:
        steps = jnp.exp(jax.random.uniform(jax.random.fold_in(own, position), (shards_of,), jnp.float32, smallest / len(cuts), largest / len(cuts)))
        factor_of = factor_of * jnp.repeat(steps, dims[position] // shards_of).reshape([-1 if axis == position else 1 for axis in range(len(dims))])
    return factor_of


def bell_draw(stream_key, dims, scale, most, cuts=(), held_as=jnp.bfloat16):
    result = scale * jax.random.normal(stream_key, dims, jnp.float32)
    if cuts:
        result = result * block_levels(stream_key, dims, cuts, -0.22, 0.18)
    return jnp.clip(result, -most, most).astype(held_as)


def setup_inputs(seed: int = 0) -> dict:
    seeds = jax.random.split(jax.random.key(seed), 7)
    history = bell_draw(seeds[0], (KH, KH), KH ** -0.5, 0.0625, ((0, 8), (1, 4)))
    self_rows = bell_draw(seeds[1], (ROWS, KH), 1.0, 6.0, ((1, 8),))
    edge_rows = bell_draw(seeds[2], (ROW_T, KH), 1.0, 6.0, ((1, 4),))
    step_inv = draw_step_inv(jax.random.fold_in(seeds[6], 71), 0)
    coupling = jnp.clip(jnp.exp(jax.random.uniform(seeds[4], (ROW_T,), jnp.float32, math.log(0.1), math.log(1.0))), 0.1, 1.0)
    reach = draw_reach(jax.random.fold_in(seeds[6], 71), 0)
    return {"history": history, "self_rows": self_rows, "edge_rows": edge_rows, "step_inv": step_inv, "coupling": coupling, "reach": reach}


def screened(block_rows, weights):
    square = block_rows * block_rows
    return weights[:, None] * block_rows * square / (1.0 + square)


def reference(history, self_rows, edge_rows, step_inv, coupling, reach):
    slab_rows = KH // N_HIST
    past_slab = slab_rows // ROW_T
    shards = history.reshape(N_HIST, slab_rows, KH)
    starts = jnp.arange(N_HIST, dtype=jnp.int32) * past_slab
    weights = jnp.tile(coupling, TPB)
    sigma_rows = self_rows
    green_now = edge_rows.astype(jnp.float32)
    finished = None
    for moment in range(NBLK):
        limit_row = reach[moment]
        pieces = jnp.moveaxis(sigma_rows.reshape(ROWS, N_HIST, slab_rows), 1, 0)

        def add_shard(running, inputs):
            rows_hist, left_rows, first_past = inputs
            past_ids = first_past + jnp.arange(past_slab, dtype=jnp.int32)
            live_mask = past_ids[:, None] < limit_row[None, :]
            masked = jnp.where(live_mask[:, None, :, None], rows_hist.reshape(past_slab, ROW_T, P_SIZE, ROW_T),
                               jnp.zeros((), rows_hist.dtype)).reshape(slab_rows, KH)
            shard_term = jnp.dot(left_rows.astype(jnp.float32), masked.astype(jnp.float32),
                                 precision=lax.Precision.HIGHEST, preferred_element_type=jnp.float32)
            rounded = lax.optimization_barrier(shard_term.astype(jnp.bfloat16))
            return running + rounded.astype(jnp.float32), None

        integral, _ = lax.scan(add_shard, jnp.zeros((ROWS, KH), jnp.float32), (shards, pieces, starts))
        rows_out = []
        for step_number in range(TPB):
            source = green_now + integral[step_number * ROW_T:(step_number + 1) * ROW_T]
            green_now = jnp.dot(step_inv, source, precision=lax.Precision.HIGHEST,
                                preferred_element_type=jnp.float32)
            rows_out.append(green_now)
        block_rows = jnp.concatenate(rows_out, 0)
        if moment + 1 < NBLK:
            sigma_rows = screened(block_rows, weights).astype(jnp.bfloat16)
        else:
            finished = block_rows.astype(jnp.bfloat16)
    return finished
```

```python
import functools

import jax
import jax.numpy as jnp
from jax import lax
from jax.experimental import pallas as pl
from jax.experimental.pallas import tpu as pltpu
from jax.sharding import PartitionSpec as P

MESH = pl.DeviceIdType.MESH
CORES = 2
LANES = 128
BF16 = jnp.bfloat16
F32 = jnp.float32


def kernel(dims, hist_ref, self_ref, edge_ref, inv_ref, coup_ref, reach_ref, out_ref,
           masked, psend, pown, arecv, presum, rrecv, acc, green, weights, piece, relay, sig,
           a0_s, a0_r, a1_s, a1_r, z_s, z_r, home_s, fwd_s, sig_r, ag_s, ag_r, mg_s, mg_r):
    chips, planes, owners, width, row_t, steps, blocks = dims
    slab, cols = hist_ref.shape
    half = cols // CORES
    past, tiles = slab // row_t, cols // row_t
    h = lax.axis_index("hist")
    s = lax.axis_index("second")
    q, c = h // CORES, lax.rem(h, CORES)
    mate = q * CORES + 1 - c
    pending = []

    def when(cond, fn):
        if cond is True:
            fn()
        else:
            pl.when(cond)(fn)

    def both(*conds):
        total = True
        for cond in conds:
            if cond is True:
                continue
            total = cond if total is True else jnp.logical_and(total, cond)
        return total

    def owns(chip):
        return True if owners == chips else chip < owners

    def live(hh, plane):
        return hh * past < (plane + 1) * tiles - 1 + 2 * (blocks - 1) + 4

    def remote(src, dst, send, recv, hist_to, second_to):
        return pltpu.make_async_remote_copy(
            src_ref=src, dst_ref=dst, send_sem=send, recv_sem=recv,
            device_id={"hist": hist_to, "second": second_to}, device_id_type=MESH)

    def start(cond, copy):
        when(cond, copy.start)
        pending.append((cond, copy))

    live_me, live_mate = live(h, s), live(mate, s)
    mine = owns(q)

    barrier = pltpu.get_barrier_semaphore()

    def greet(hist_to, second_to):
        pl.semaphore_signal(barrier, inc=1, device_id={"hist": hist_to, "second": second_to},
                            device_id_type=MESH)

    greet(mate, s)
    for d in range(1, chips):
        greet(lax.rem(q + d, chips) * CORES + c, s)
    for d in range(1, planes):
        greet(h, lax.rem(s + d, planes))

    def chip_cols(chip):
        return pl.ds(pl.multiple_of(chip * width, width), width)

    def own_cols(chip, core):
        return pl.ds(pl.multiple_of(core * half + chip * width, width), width)

    def make_mask(b):
        def work():
            def body(ct, carry):
                limit = reach_ref[b, s * tiles + ct]
                at = pl.ds(pl.multiple_of(ct * row_t, row_t), row_t)
                for kt in range(past):
                    keep = jnp.where(h * past + kt < limit, 1.0, 0.0).astype(F32)
                    rows = slice(kt * row_t, (kt + 1) * row_t)
                    masked[b, rows, at] = hist_ref[rows, at] * jnp.full((row_t, row_t), keep, F32).astype(BF16)
                return carry
            lax.fori_loop(0, tiles, body, 0)
        when(live_me, work)

    def product(b, i, dst, core):
        idx = b * steps + i
        chunk = 256

        def body(t, carry):
            left = self_ref[i * row_t:(i + 1) * row_t, :] if b == 0 else sig[idx - steps]
            at = pl.ds(pl.multiple_of(core * half + t * chunk, chunk), chunk)
            to = pl.ds(pl.multiple_of(t * chunk, chunk), chunk)
            dst[idx, :, to] = jnp.dot(left, masked[b, :, at], preferred_element_type=F32).astype(BF16)
            return carry
        lax.fori_loop(0, half // chunk, body, 0)

    def a0_copy(idx):
        return remote(psend.at[idx], arecv.at[idx], a0_s.at[idx], a0_r.at[idx], mate, s)

    def sig_wait(idx):
        for e in range(1, chips):
            p = lax.rem(q + e, chips)

            def wait(p=p):
                spot = sig.at[idx, :, chip_cols(p)]
                remote(spot, spot, home_s.at[idx], sig_r.at[idx, p], p * CORES + c, s).wait_recv()
            when(owns(p), wait)

    def stage_product(b, i):
        idx = b * steps + i

        def first():
            if b:
                sig_wait(idx - steps)
            product(b, i, psend, 1 - c)
        when(live_me, first)
        if idx == 0:
            pl.semaphore_wait(barrier, 1 + (chips - 1) + (planes - 1))
        start(live_me, a0_copy(idx))
        when(live_me, lambda: product(b, i, pown, c))

    def a1_copy(idx, d):
        to = lax.rem(q + d, chips)
        return remote(presum.at[idx, :, chip_cols(to)], rrecv.at[idx, d - 1],
                      a1_s.at[idx, d - 1], a1_r.at[idx, d - 1], to * CORES + c, s)

    def stage_pair(b, i):
        idx = b * steps + i

        def pair():
            a0_copy(idx).wait_recv()
            presum[idx] = (pown[idx].astype(F32) + arecv[idx].astype(F32)).astype(BF16)

        def alone():
            presum[idx] = pown[idx]

        def other():
            a0_copy(idx).wait_recv()
            presum[idx] = arecv[idx]
        no_me, no_mate = jnp.logical_not(live_me), jnp.logical_not(live_mate)
        when(both(live_me, live_mate), pair)
        when(both(live_me, no_mate), alone)
        when(both(no_me, live_mate), other)
        for d in range(1, chips):
            to = lax.rem(q + d, chips)
            start(both(live(q * CORES, s), owns(to)), a1_copy(idx, d))

    def stage_reduce(b, i):
        idx = b * steps + i
        last = b + 1 == blocks

        def init():
            acc[...] = jnp.zeros_like(acc)

        def own():
            acc[...] = presum[idx, :, chip_cols(q)].astype(F32)

        when(mine, init)
        when(both(mine, live(q * CORES, s)), own)
        for d in range(1, chips):
            src = lax.rem(q + chips - d, chips)

            def add(d=d):
                a1_copy(idx, d).wait_recv()
                acc[...] += rrecv[idx, d - 1].astype(F32)
            when(both(mine, live(src * CORES, s)), add)

        def step():
            fresh = jnp.dot(inv_ref[...], green[...] + acc[...], precision=lax.Precision.HIGHEST,
                            preferred_element_type=F32)
            green[...] = fresh
            if last:
                out_ref[i * row_t:(i + 1) * row_t, own_cols(q, c)] = fresh.astype(BF16)
            else:
                square = fresh * fresh
                piece[idx] = (weights[...] * fresh * square / (1.0 + square)).astype(BF16)
        when(mine, step)
        if last:
            rows = slice(i * row_t, (i + 1) * row_t)
            spot = out_ref.at[rows, own_cols(q, c)]
            for d in range(1, chips):
                start(mine, remote(spot, spot, ag_s.at[i, d - 1], ag_r.at[i, d - 1],
                                   lax.rem(q + d, chips) * CORES + c, s))
            start(mine, remote(spot, spot, mg_s.at[i, 0], mg_r.at[i, 0], mate, s))
            return
        for d in range(planes - 1, 0, -1):
            to = lax.rem(s + d, planes)
            start(both(mine, live(s * CORES + c, to)),
                  remote(piece.at[idx], relay.at[idx, d - 1], z_s.at[idx, d - 1], z_r.at[idx, d - 1], h, to))
        spot = sig.at[idx, :, chip_cols(q)]
        start(both(mine, q != s), remote(piece.at[idx], spot, home_s.at[idx], sig_r.at[idx, q], s * CORES + c, s))

        def keep():
            sig[idx, :, chip_cols(q)] = piece[idx]
        when(both(mine, q == s), keep)

    def stage_forward(b, i):
        idx = b * steps + i
        for d in range(1, planes):
            src = lax.rem(s + planes - d, planes)
            used = both(mine, live(src * CORES + c, s))
            landed = relay.at[idx, d - 1]

            def wait(landed=landed, src=src, d=d):
                remote(landed, landed, z_s.at[idx, d - 1], z_r.at[idx, d - 1], h, src).wait_recv()
            when(used, wait)
            start(both(used, q != src),
                  remote(landed, sig.at[idx, :, chip_cols(q)], fwd_s.at[idx, d - 1], sig_r.at[idx, q],
                         src * CORES + c, s))

            def keep(d=d):
                sig[idx, :, chip_cols(q)] = relay[idx, d - 1]
            when(both(used, q == src), keep)

    def stage_gather(i):
        rows = slice(i * row_t, (i + 1) * row_t)
        for d in range(1, chips):
            src = lax.rem(q + chips - d, chips)
            spot = out_ref.at[rows, own_cols(src, c)]

            def wait(spot=spot, src=src, d=d):
                remote(spot, spot, ag_s.at[i, d - 1], ag_r.at[i, d - 1], src * CORES + c, s).wait_recv()
            when(owns(src), wait)
            start(owns(src), remote(spot, spot, mg_s.at[i, d], mg_r.at[i, d], mate, s))

    def stage_close(i):
        rows = slice(i * row_t, (i + 1) * row_t)
        for d in range(chips):
            src = lax.rem(q + chips - d, chips)

            def wait(src=src, d=d):
                spot = out_ref.at[rows, own_cols(src, 1 - c)]
                remote(spot, spot, mg_s.at[i, d], mg_r.at[i, d], mate, s).wait_recv()
            when(owns(src), wait)

    make_mask(0)
    for b in range(blocks):
        for i in range(steps):
            stage_product(b, i)
        for i in range(steps):
            stage_pair(b, i)
        if b == 0:
            row = lax.broadcasted_iota(jnp.int32, (row_t, row_t), 0)
            col = lax.broadcasted_iota(jnp.int32, (row_t, row_t), 1)
            spread = jnp.where(row == col, jnp.broadcast_to(coup_ref[...], (row_t, row_t)), 0.0)
            weights[...] = jnp.broadcast_to(jnp.sum(spread, axis=1, keepdims=True), weights.shape)

            def first_green():
                green[...] = edge_ref[:, own_cols(q, c)].astype(F32)
            when(mine, first_green)
        if b + 1 < blocks:
            make_mask(b + 1)
        for i in range(steps):
            stage_reduce(b, i)
        for i in range(steps):
            if b + 1 < blocks:
                stage_forward(b, i)
            else:
                stage_gather(i)
    for i in range(steps):
        stage_close(i)
    for cond, copy in pending:
        when(cond, copy.wait_send)


def local(hist_count, second_count, history, self_rows, edge_rows, step_inv, coupling, reach):
    slab, cols = history.shape
    row_t = step_inv.shape[0]
    steps = self_rows.shape[0] // row_t
    blocks = reach.shape[0]
    chips, planes = hist_count // CORES, second_count
    half = cols // CORES
    owners = min(chips, half // LANES)
    width = half // owners
    assert chips == planes and half == slab
    dims = (chips, planes, owners, width, row_t, steps, blocks)
    n, m = blocks * steps, (blocks - 1) * steps
    vmem = pl.BlockSpec(memory_space=pltpu.VMEM)
    dma = pltpu.SemaphoreType.DMA
    return pl.pallas_call(
        functools.partial(kernel, dims),
        out_shape=jax.ShapeDtypeStruct((steps * row_t, cols), BF16),
        in_specs=[vmem] * 5 + [pl.BlockSpec(memory_space=pltpu.SMEM)],
        out_specs=vmem,
        scratch_shapes=[
            pltpu.VMEM((blocks, slab, cols), BF16),
            pltpu.VMEM((n, row_t, half), BF16),
            pltpu.VMEM((n, row_t, half), BF16),
            pltpu.VMEM((n, row_t, half), BF16),
            pltpu.VMEM((n, row_t, half), BF16),
            pltpu.VMEM((n, chips - 1, row_t, width), BF16),
            pltpu.VMEM((row_t, width), F32),
            pltpu.VMEM((row_t, width), F32),
            pltpu.VMEM((row_t, width), F32),
            pltpu.VMEM((m, row_t, width), BF16),
            pltpu.VMEM((m, planes - 1, row_t, width), BF16),
            pltpu.VMEM((m, row_t, slab), BF16),
            dma((n,)), dma((n,)),
            dma((n, chips - 1)), dma((n, chips - 1)),
            dma((m, planes - 1)), dma((m, planes - 1)),
            dma((m,)), dma((m, planes - 1)), dma((m, chips)),
            dma((steps, chips - 1)), dma((steps, chips - 1)),
            dma((steps, chips)), dma((steps, chips)),
        ],
        compiler_params=pltpu.CompilerParams(
            collective_id=0, has_side_effects=True, vmem_limit_bytes=48 * 1024 * 1024),
        cost_estimate=pl.CostEstimate(
            flops=2 * blocks * steps * row_t * slab * cols, bytes_accessed=2 * slab * cols, transcendentals=0),
    )(history, self_rows, edge_rows, step_inv, coupling.reshape(1, row_t), reach)


def solution(mesh):
    placed = (P("hist", "second"), P(None, "hist"), P(None, "second"), P(), P(), P())
    return jax.shard_map(
        functools.partial(local, mesh.shape["hist"], mesh.shape["second"]),
        mesh=mesh, in_specs=placed, out_specs=P(None, "second"), check_vma=False
    )
```

```python
import functools

import jax
import jax.numpy as jnp
from jax import lax
from jax.experimental import pallas as pl
from jax.experimental.pallas import tpu as pltpu
from jax.sharding import PartitionSpec as P

MESH = pl.DeviceIdType.MESH
CORES = 2
LANES = 128
BF16 = jnp.bfloat16
F32 = jnp.float32


def kernel(dims, hist_hbm, self_hbm, edge_hbm, inv_hbm, coup_hbm, reach_ref, out_ref,
           hist_ref, self_ref, edge_ref, inv_ref, coup_ref, load_s, masked, psend, pown, arecv, presum, rrecv, acc, green, weights, piece, relay, sig,
           a0_s, a0_r, a1_s, a1_r, z_s, z_r, home_s, fwd_s, sig_r, ag_s, ag_r, mg_s, mg_r):
    chips, planes, owners, width, row_t, steps, blocks, below = dims
    slab, cols = hist_hbm.shape
    half = cols // CORES
    past, tiles = slab // row_t, cols // row_t
    h = lax.axis_index("hist")
    s = lax.axis_index("second")
    q, c = h // CORES, lax.rem(h, CORES)
    mate = q * CORES + 1 - c
    pending = []

    def when(cond, fn):
        if cond is True:
            fn()
        else:
            pl.when(cond)(fn)

    def both(*conds):
        total = True
        for cond in conds:
            if cond is True:
                continue
            total = cond if total is True else jnp.logical_and(total, cond)
        return total

    def owns(chip):
        return True if owners == chips else chip < owners

    def live(hh, plane):
        return hh * past < (plane + 1) * tiles - 1 + 2 * (blocks - 1) + 4

    def remote(src, dst, send, recv, hist_to, second_to):
        return pltpu.make_async_remote_copy(
            src_ref=src, dst_ref=dst, send_sem=send, recv_sem=recv,
            device_id={"hist": hist_to, "second": second_to}, device_id_type=MESH)

    def start(cond, copy):
        when(cond, copy.start)
        pending.append((cond, copy))

    live_me, live_mate = live(h, s), live(mate, s)
    mine = owns(q)

    def half_load(core, n):
        at = pl.ds(pl.multiple_of(core * half, half), half)
        return pltpu.make_async_copy(hist_hbm.at[:, at], hist_ref.at[:, at], load_s.at[n])

    load_first, load_second = half_load(1 - c, 0), half_load(c, 1)
    load_self = pltpu.make_async_copy(self_hbm, self_ref, load_s.at[2])
    edge_at = pl.ds(pl.multiple_of(c * half, half), half)
    load_small = [
        pltpu.make_async_copy(edge_hbm.at[:, edge_at], edge_ref, load_s.at[3]),
        pltpu.make_async_copy(inv_hbm, inv_ref, load_s.at[4]),
        pltpu.make_async_copy(coup_hbm, coup_ref, load_s.at[5]),
    ]
    for load in [load_first, load_self, load_second] + load_small:
        load.start()

    barrier = pltpu.get_barrier_semaphore()

    def greet(hist_to, second_to):
        pl.semaphore_signal(barrier, inc=1, device_id={"hist": hist_to, "second": second_to},
                            device_id_type=MESH)

    greet(mate, s)
    for d in range(1, chips):
        greet(lax.rem(q + d, chips) * CORES + c, s)
    for d in range(1, planes):
        greet(h, lax.rem(s + d, planes))

    def chip_cols(chip):
        return pl.ds(pl.multiple_of(chip * width, width), width)

    def own_cols(chip, core):
        return pl.ds(pl.multiple_of(core * half + chip * width, width), width)

    def make_mask(b, core):
        def work():
            def body(ct, carry):
                tile = core * (tiles // CORES) + ct
                limit = reach_ref[b, s * tiles + tile]
                at = pl.ds(pl.multiple_of(tile * row_t, row_t), row_t)
                for kt in range(past):
                    keep = jnp.where(h * past + kt < limit, 1.0, 0.0).astype(F32)
                    rows = slice(kt * row_t, (kt + 1) * row_t)
                    masked[b, rows, at] = hist_ref[rows, at] * jnp.full((row_t, row_t), keep, F32).astype(BF16)
                return carry
            lax.fori_loop(0, tiles // CORES, body, 0)
        when(live_me, work)

    def product(b, i, dst, core):
        idx = b * steps + i
        chunk = 256

        def body(t, carry):
            left = self_ref[i * row_t:(i + 1) * row_t, :] if b == 0 else sig[idx - steps]
            at = pl.ds(pl.multiple_of(core * half + t * chunk, chunk), chunk)
            to = pl.ds(pl.multiple_of(t * chunk, chunk), chunk)
            dst[idx, :, to] = jnp.dot(left, masked[b, :, at], preferred_element_type=F32).astype(BF16)
            return carry
        lax.fori_loop(0, half // chunk, body, 0)

    def a0_copy(idx):
        return remote(psend.at[idx], arecv.at[idx], a0_s.at[idx], a0_r.at[idx], mate, s)

    def sig_wait(idx):
        for e in range(1, chips):
            p = lax.rem(q + e, chips)

            def wait(p=p):
                spot = sig.at[idx, :, chip_cols(p)]
                remote(spot, spot, home_s.at[idx], sig_r.at[idx, p], p * CORES + c, s).wait_recv()
            when(owns(p), wait)

    def stage_product(b, i):
        idx = b * steps + i

        def first():
            if b:
                sig_wait(idx - steps)
            product(b, i, psend, 1 - c)
        when(live_me, first)
        if idx == 0:
            pl.semaphore_wait(barrier, 1 + (chips - 1) + (planes - 1))
        start(live_me, a0_copy(idx))
        when(live_me, lambda: product(b, i, pown, c))

    def a1_copy(idx, d):
        to = lax.rem(q + d, chips)
        return remote(presum.at[idx, :, chip_cols(to)], rrecv.at[idx, d - 1],
                      a1_s.at[idx, d - 1], a1_r.at[idx, d - 1], to * CORES + c, s)

    def stage_pair(b, i):
        idx = b * steps + i

        def pair():
            a0_copy(idx).wait_recv()
            presum[idx] = (pown[idx].astype(F32) + arecv[idx].astype(F32)).astype(BF16)

        def alone():
            presum[idx] = pown[idx]

        def other():
            a0_copy(idx).wait_recv()
            presum[idx] = arecv[idx]
        no_me, no_mate = jnp.logical_not(live_me), jnp.logical_not(live_mate)
        when(both(live_me, live_mate), pair)
        when(both(live_me, no_mate), alone)
        when(both(no_me, live_mate), other)
        for d in range(1, chips):
            to = lax.rem(q + d, chips)
            start(both(live(q * CORES, s), owns(to)), a1_copy(idx, d))

    def stage_reduce(b, i):
        idx = b * steps + i
        last = b + 1 == blocks

        def init():
            acc[...] = jnp.zeros_like(acc)

        def own():
            acc[...] = presum[idx, :, chip_cols(q)].astype(F32)

        when(mine, init)
        when(both(mine, live(q * CORES, s)), own)
        for d in range(1, chips):
            src = lax.rem(q + chips - d, chips)

            def add(d=d):
                a1_copy(idx, d).wait_recv()
                acc[...] += rrecv[idx, d - 1].astype(F32)
            when(both(mine, live(src * CORES, s)), add)

        def step():
            fresh = jnp.dot(inv_ref[...], green[...] + acc[...], precision=lax.Precision.HIGHEST,
                            preferred_element_type=F32)
            green[...] = fresh
            if last:
                out_ref[i * row_t:(i + 1) * row_t, own_cols(q, c)] = fresh.astype(BF16)
            else:
                square = fresh * fresh
                piece[idx] = (weights[...] * fresh * square / (1.0 + square)).astype(BF16)
        when(mine, step)
        if last:
            rows = slice(i * row_t, (i + 1) * row_t)
            spot = out_ref.at[rows, own_cols(q, c)]
            for d in range(1, chips):
                start(mine, remote(spot, spot, ag_s.at[i, d - 1], ag_r.at[i, d - 1],
                                   lax.rem(q + d, chips) * CORES + c, s))
            start(mine, remote(spot, spot, mg_s.at[i, 0], mg_r.at[i, 0], mate, s))
            return
        start(both(mine, s + 1 < planes), up_copy(idx, 0))
        for e in range(1, below + 1):
            start(both(mine, s >= e, live(s * CORES + c, s - e)), down_copy(idx, e, s - e))
        spot = sig.at[idx, :, chip_cols(q)]
        start(both(mine, q != s), remote(piece.at[idx], spot, home_s.at[idx], sig_r.at[idx, q], s * CORES + c, s))

        def keep():
            sig[idx, :, chip_cols(q)] = piece[idx]
        when(both(mine, q == s), keep)

    def up_copy(idx, d):
        src = piece.at[idx] if d == 0 else relay.at[idx, d - 1]
        return remote(src, relay.at[idx, d], z_s.at[idx, d], z_r.at[idx, d], h, lax.rem(s + 1, planes))

    def down_copy(idx, e, to):
        slot = planes - 2 + e
        return remote(piece.at[idx], relay.at[idx, slot], z_s.at[idx, slot], z_r.at[idx, slot],
                      h, lax.rem(to + planes, planes))

    def pass_on(idx, slot, src, used):
        start(both(used, q != src),
              remote(relay.at[idx, slot], sig.at[idx, :, chip_cols(q)], fwd_s.at[idx, slot], sig_r.at[idx, q],
                     lax.rem(src + planes, planes) * CORES + c, s))

        def keep():
            sig[idx, :, chip_cols(q)] = relay[idx, slot]
        when(both(used, q == src), keep)

    def stage_up(b, i, d):
        idx = b * steps + i
        used = both(mine, s >= d)

        def wait():
            landed = relay.at[idx, d - 1]
            remote(landed, landed, z_s.at[idx, d - 1], z_r.at[idx, d - 1], h, lax.rem(s + planes - 1, planes)).wait_recv()
        when(used, wait)
        if d < planes - 1:
            start(both(used, s + 1 < planes), up_copy(idx, d))
        pass_on(idx, d - 1, s - d, used)

    def stage_down(b, i):
        idx = b * steps + i
        for e in range(1, below + 1):
            used = both(mine, s + e < planes, live((s + e) * CORES + c, s))
            when(used, down_copy(idx, e, s + e).wait_recv)
            pass_on(idx, planes - 2 + e, s + e, used)

    def forward_first(b, i):
        stage_up(b, i, 1)

    def forward_rest(b, i):
        for d in range(2, planes):
            stage_up(b, i, d)
        stage_down(b, i)

    def stage_gather(i):
        rows = slice(i * row_t, (i + 1) * row_t)
        for d in range(1, chips):
            src = lax.rem(q + chips - d, chips)
            spot = out_ref.at[rows, own_cols(src, c)]

            def wait(spot=spot, src=src, d=d):
                remote(spot, spot, ag_s.at[i, d - 1], ag_r.at[i, d - 1], src * CORES + c, s).wait_recv()
            when(owns(src), wait)
            start(owns(src), remote(spot, spot, mg_s.at[i, d], mg_r.at[i, d], mate, s))

    def stage_close(i):
        rows = slice(i * row_t, (i + 1) * row_t)
        for d in range(chips):
            src = lax.rem(q + chips - d, chips)

            def wait(src=src, d=d):
                spot = out_ref.at[rows, own_cols(src, 1 - c)]
                remote(spot, spot, mg_s.at[i, d], mg_r.at[i, d], mate, s).wait_recv()
            when(owns(src), wait)

    load_first.wait()
    load_self.wait()
    make_mask(0, 1 - c)
    load_second.wait()
    make_mask(0, c)
    for i in range(steps):
        stage_product(0, i)
    for i in range(steps):
        stage_pair(0, i)
    for load in load_small:
        load.wait()
    row = lax.broadcasted_iota(jnp.int32, (row_t, row_t), 0)
    col = lax.broadcasted_iota(jnp.int32, (row_t, row_t), 1)
    spread = jnp.where(row == col, jnp.broadcast_to(coup_ref[...], (row_t, row_t)), 0.0)
    weights[...] = jnp.broadcast_to(jnp.sum(spread, axis=1, keepdims=True), weights.shape)

    def first_green():
        green[...] = edge_ref[:, chip_cols(q)].astype(F32)
    when(mine, first_green)
    for i in range(steps):
        stage_reduce(0, i)
    for b in range(1, blocks):
        make_mask(b, 0)
        make_mask(b, 1)
        forward_first(b - 1, 0)
        forward_rest(b - 1, 0)
        for i in range(steps):
            if i + 1 < steps:
                forward_first(b - 1, i + 1)
            stage_product(b, i)
            stage_pair(b, i)
            if i + 1 < steps:
                forward_rest(b - 1, i + 1)
            if b + 1 == blocks and i:
                stage_gather(i - 1)
            stage_reduce(b, i)
    stage_gather(steps - 1)
    for i in range(steps):
        stage_close(i)
    for cond, copy in pending:
        when(cond, copy.wait_send)


def local(hist_count, second_count, history, self_rows, edge_rows, step_inv, coupling, reach):
    slab, cols = history.shape
    row_t = step_inv.shape[0]
    steps = self_rows.shape[0] // row_t
    blocks = reach.shape[0]
    chips, planes = hist_count // CORES, second_count
    half = cols // CORES
    owners = min(chips, half // LANES)
    width = half // owners
    assert chips == planes and half == slab
    past, tiles = slab // row_t, cols // row_t
    below = (tiles + 2 + 2 * (blocks - 1)) // (CORES * past)
    slots = planes - 1 + below
    dims = (chips, planes, owners, width, row_t, steps, blocks, below)
    n, m = blocks * steps, (blocks - 1) * steps
    vmem = pl.BlockSpec(memory_space=pltpu.VMEM)
    dma = pltpu.SemaphoreType.DMA
    return pl.pallas_call(
        functools.partial(kernel, dims),
        out_shape=jax.ShapeDtypeStruct((steps * row_t, cols), BF16),
        in_specs=[pl.BlockSpec(memory_space=pl.ANY)] * 5 + [pl.BlockSpec(memory_space=pltpu.SMEM)],
        out_specs=vmem,
        scratch_shapes=[
            pltpu.VMEM((slab, cols), BF16),
            pltpu.VMEM(self_rows.shape, BF16),
            pltpu.VMEM((row_t, half), BF16),
            pltpu.VMEM((row_t, row_t), F32),
            pltpu.VMEM((1, row_t), F32),
            dma((6,)),
            pltpu.VMEM((blocks, slab, cols), BF16),
            pltpu.VMEM((n, row_t, half), BF16),
            pltpu.VMEM((n, row_t, half), BF16),
            pltpu.VMEM((n, row_t, half), BF16),
            pltpu.VMEM((n, row_t, half), BF16),
            pltpu.VMEM((n, chips - 1, row_t, width), BF16),
            pltpu.VMEM((row_t, width), F32),
            pltpu.VMEM((row_t, width), F32),
            pltpu.VMEM((row_t, width), F32),
            pltpu.VMEM((m, row_t, width), BF16),
            pltpu.VMEM((m, slots, row_t, width), BF16),
            pltpu.VMEM((m, row_t, slab), BF16),
            dma((n,)), dma((n,)),
            dma((n, chips - 1)), dma((n, chips - 1)),
            dma((m, slots)), dma((m, slots)),
            dma((m,)), dma((m, slots)), dma((m, chips)),
            dma((steps, chips - 1)), dma((steps, chips - 1)),
            dma((steps, chips)), dma((steps, chips)),
        ],
        compiler_params=pltpu.CompilerParams(
            collective_id=0, has_side_effects=True, vmem_limit_bytes=56 * 1024 * 1024),
        cost_estimate=pl.CostEstimate(
            flops=2 * blocks * steps * row_t * slab * cols, bytes_accessed=2 * slab * cols, transcendentals=0),
    )(history, self_rows, edge_rows, step_inv, coupling.reshape(1, row_t), reach)


def solution(mesh):
    placed = (P("hist", "second"), P(None, "hist"), P(None, "second"), P(), P(), P())
    return jax.shard_map(
        functools.partial(local, mesh.shape["hist"], mesh.shape["second"]),
        mesh=mesh, in_specs=placed, out_specs=P(None, "second"), check_vma=False
    )
```

```python
import functools

import jax
import jax.numpy as jnp
from jax import lax
from jax.experimental import pallas as pl
from jax.experimental.pallas import tpu as pltpu
from jax.sharding import PartitionSpec as P

MESH = pl.DeviceIdType.MESH
CORES = 2
LANES = 128
BF16 = jnp.bfloat16
F32 = jnp.float32


def kernel(dims, hist_ref, self_ref, edge_ref, inv_ref, coup_ref, reach_ref, out_ref,
           masked, psend, pown, arecv, presum, rrecv, acc, green, weights, piece, relay, sig,
           a0_s, a0_r, a1_s, a1_r, z_s, z_r, home_s, fwd_s, sig_r, ag_s, ag_r, mg_s, mg_r):
    chips, planes, owners, width, row_t, steps, blocks = dims
    slab, cols = hist_ref.shape
    half = cols // CORES
    past, tiles = slab // row_t, cols // row_t
    h = lax.axis_index("hist")
    s = lax.axis_index("second")
    q, c = h // CORES, lax.rem(h, CORES)
    mate = q * CORES + 1 - c
    pending = []

    def when(cond, fn):
        if cond is True:
            fn()
        else:
            pl.when(cond)(fn)

    def both(*conds):
        total = True
        for cond in conds:
            if cond is True:
                continue
            total = cond if total is True else jnp.logical_and(total, cond)
        return total

    def owns(chip):
        return True if owners == chips else chip < owners

    def live(hh, plane):
        return hh * past < (plane + 1) * tiles - 1 + 2 * (blocks - 1) + 4

    def remote(src, dst, send, recv, hist_to, second_to):
        return pltpu.make_async_remote_copy(
            src_ref=src, dst_ref=dst, send_sem=send, recv_sem=recv,
            device_id={"hist": hist_to, "second": second_to}, device_id_type=MESH)

    def start(cond, copy):
        when(cond, copy.start)
        pending.append((cond, copy))

    live_me, live_mate = live(h, s), live(mate, s)
    mine = owns(q)

    barrier = pltpu.get_barrier_semaphore()

    def greet(hist_to, second_to):
        pl.semaphore_signal(barrier, inc=1, device_id={"hist": hist_to, "second": second_to},
                            device_id_type=MESH)

    greet(mate, s)
    for d in range(1, chips):
        greet(lax.rem(q + d, chips) * CORES + c, s)
    for d in range(1, planes):
        greet(h, lax.rem(s + d, planes))

    def chip_cols(chip):
        return pl.ds(pl.multiple_of(chip * width, width), width)

    def own_cols(chip, core):
        return pl.ds(pl.multiple_of(core * half + chip * width, width), width)

    def make_mask(b):
        def work():
            def body(ct, carry):
                limit = reach_ref[b, s * tiles + ct]
                at = pl.ds(pl.multiple_of(ct * row_t, row_t), row_t)
                for kt in range(past):
                    keep = jnp.where(h * past + kt < limit, 1.0, 0.0).astype(F32)
                    rows = slice(kt * row_t, (kt + 1) * row_t)
                    masked[b, rows, at] = hist_ref[rows, at] * jnp.full((row_t, row_t), keep, F32).astype(BF16)
                return carry
            lax.fori_loop(0, tiles, body, 0)
        when(live_me, work)

    def product(b, i, dst, core):
        idx = b * steps + i
        chunk = 256

        def body(t, carry):
            left = self_ref[i * row_t:(i + 1) * row_t, :] if b == 0 else sig[idx - steps]
            at = pl.ds(pl.multiple_of(core * half + t * chunk, chunk), chunk)
            to = pl.ds(pl.multiple_of(t * chunk, chunk), chunk)
            dst[idx, :, to] = jnp.dot(left, masked[b, :, at], preferred_element_type=F32).astype(BF16)
            return carry
        lax.fori_loop(0, half // chunk, body, 0)

    def a0_copy(idx):
        return remote(psend.at[idx], arecv.at[idx], a0_s.at[idx], a0_r.at[idx], mate, s)

    def sig_wait(idx):
        for e in range(1, chips):
            p = lax.rem(q + e, chips)

            def wait(p=p):
                spot = sig.at[idx, :, chip_cols(p)]
                remote(spot, spot, home_s.at[idx], sig_r.at[idx, p], p * CORES + c, s).wait_recv()
            when(owns(p), wait)

    def stage_product(b, i):
        idx = b * steps + i

        def first():
            if b:
                sig_wait(idx - steps)
            product(b, i, psend, 1 - c)
        when(live_me, first)
        if idx == 0:
            pl.semaphore_wait(barrier, 1 + (chips - 1) + (planes - 1))
        start(live_me, a0_copy(idx))
        when(live_me, lambda: product(b, i, pown, c))

    def a1_copy(idx, d):
        to = lax.rem(q + d, chips)
        return remote(presum.at[idx, :, chip_cols(to)], rrecv.at[idx, d - 1],
                      a1_s.at[idx, d - 1], a1_r.at[idx, d - 1], to * CORES + c, s)

    def stage_pair(b, i):
        idx = b * steps + i

        def pair():
            a0_copy(idx).wait_recv()
            presum[idx] = (pown[idx].astype(F32) + arecv[idx].astype(F32)).astype(BF16)

        def alone():
            presum[idx] = pown[idx]

        def other():
            a0_copy(idx).wait_recv()
            presum[idx] = arecv[idx]
        no_me, no_mate = jnp.logical_not(live_me), jnp.logical_not(live_mate)
        when(both(live_me, live_mate), pair)
        when(both(live_me, no_mate), alone)
        when(both(no_me, live_mate), other)
        for d in range(1, chips):
            to = lax.rem(q + d, chips)
            start(both(live(q * CORES, s), owns(to)), a1_copy(idx, d))

    def stage_reduce(b, i):
        idx = b * steps + i
        last = b + 1 == blocks

        def init():
            acc[...] = jnp.zeros_like(acc)

        def own():
            acc[...] = presum[idx, :, chip_cols(q)].astype(F32)

        when(mine, init)
        when(both(mine, live(q * CORES, s)), own)
        for d in range(1, chips):
            src = lax.rem(q + chips - d, chips)

            def add(d=d):
                a1_copy(idx, d).wait_recv()
                acc[...] += rrecv[idx, d - 1].astype(F32)
            when(both(mine, live(src * CORES, s)), add)

        def step():
            fresh = jnp.dot(inv_ref[...], green[...] + acc[...], precision=lax.Precision.HIGHEST,
                            preferred_element_type=F32)
            green[...] = fresh
            if last:
                out_ref[i * row_t:(i + 1) * row_t, own_cols(q, c)] = fresh.astype(BF16)
            else:
                square = fresh * fresh
                piece[idx] = (weights[...] * fresh * square / (1.0 + square)).astype(BF16)
        when(mine, step)
        if last:
            rows = slice(i * row_t, (i + 1) * row_t)
            spot = out_ref.at[rows, own_cols(q, c)]
            for d in range(1, chips):
                start(mine, remote(spot, spot, ag_s.at[i, d - 1], ag_r.at[i, d - 1],
                                   lax.rem(q + d, chips) * CORES + c, s))
            start(mine, remote(spot, spot, mg_s.at[i, 0], mg_r.at[i, 0], mate, s))
            return
        for d in range(planes - 1, 0, -1):
            to = lax.rem(s + d, planes)
            start(both(mine, live(s * CORES + c, to)),
                  remote(piece.at[idx], relay.at[idx, d - 1], z_s.at[idx, d - 1], z_r.at[idx, d - 1], h, to))
        spot = sig.at[idx, :, chip_cols(q)]
        start(both(mine, q != s), remote(piece.at[idx], spot, home_s.at[idx], sig_r.at[idx, q], s * CORES + c, s))

        def keep():
            sig[idx, :, chip_cols(q)] = piece[idx]
        when(both(mine, q == s), keep)

    def stage_forward(b, i, first, stop):
        idx = b * steps + i
        for d in range(first, stop):
            src = lax.rem(s + planes - d, planes)
            used = both(mine, live(src * CORES + c, s))
            landed = relay.at[idx, d - 1]

            def wait(landed=landed, src=src, d=d):
                remote(landed, landed, z_s.at[idx, d - 1], z_r.at[idx, d - 1], h, src).wait_recv()
            when(used, wait)
            start(both(used, q != src),
                  remote(landed, sig.at[idx, :, chip_cols(q)], fwd_s.at[idx, d - 1], sig_r.at[idx, q],
                         src * CORES + c, s))

            def keep(d=d):
                sig[idx, :, chip_cols(q)] = relay[idx, d - 1]
            when(both(used, q == src), keep)

    def stage_gather(i):
        rows = slice(i * row_t, (i + 1) * row_t)
        for d in range(1, chips):
            src = lax.rem(q + chips - d, chips)
            spot = out_ref.at[rows, own_cols(src, c)]

            def wait(spot=spot, src=src, d=d):
                remote(spot, spot, ag_s.at[i, d - 1], ag_r.at[i, d - 1], src * CORES + c, s).wait_recv()
            when(owns(src), wait)
            start(owns(src), remote(spot, spot, mg_s.at[i, d], mg_r.at[i, d], mate, s))

    def stage_close(i):
        rows = slice(i * row_t, (i + 1) * row_t)
        for d in range(chips):
            src = lax.rem(q + chips - d, chips)

            def wait(src=src, d=d):
                spot = out_ref.at[rows, own_cols(src, 1 - c)]
                remote(spot, spot, mg_s.at[i, d], mg_r.at[i, d], mate, s).wait_recv()
            when(owns(src), wait)

    make_mask(0)
    for i in range(steps):
        stage_product(0, i)
    for i in range(steps):
        stage_pair(0, i)
    row = lax.broadcasted_iota(jnp.int32, (row_t, row_t), 0)
    col = lax.broadcasted_iota(jnp.int32, (row_t, row_t), 1)
    spread = jnp.where(row == col, jnp.broadcast_to(coup_ref[...], (row_t, row_t)), 0.0)
    weights[...] = jnp.broadcast_to(jnp.sum(spread, axis=1, keepdims=True), weights.shape)

    def first_green():
        green[...] = edge_ref[:, own_cols(q, c)].astype(F32)
    when(mine, first_green)
    for b in range(1, blocks):
        for i in range(steps):
            stage_reduce(b - 1, i)
        make_mask(b)
        stage_forward(b - 1, 0, 1, planes)
        if steps > 1:
            stage_forward(b - 1, 1, 1, 2)
        stage_product(b, 0)
        stage_pair(b, 0)
        for i in range(1, steps):
            stage_forward(b - 1, i, 2 if i == 1 else 1, planes)
            stage_product(b, i)
            stage_pair(b, i)
    for i in range(steps):
        stage_reduce(blocks - 1, i)
    for i in range(steps):
        stage_gather(i)
    for i in range(steps):
        stage_close(i)
    for cond, copy in pending:
        when(cond, copy.wait_send)


def local(hist_count, second_count, history, self_rows, edge_rows, step_inv, coupling, reach):
    slab, cols = history.shape
    row_t = step_inv.shape[0]
    steps = self_rows.shape[0] // row_t
    blocks = reach.shape[0]
    chips, planes = hist_count // CORES, second_count
    half = cols // CORES
    owners = min(chips, half // LANES)
    width = half // owners
    assert chips == planes and half == slab
    dims = (chips, planes, owners, width, row_t, steps, blocks)
    n, m = blocks * steps, (blocks - 1) * steps
    vmem = pl.BlockSpec(memory_space=pltpu.VMEM)
    dma = pltpu.SemaphoreType.DMA
    return pl.pallas_call(
        functools.partial(kernel, dims),
        out_shape=jax.ShapeDtypeStruct((steps * row_t, cols), BF16),
        in_specs=[vmem] * 5 + [pl.BlockSpec(memory_space=pltpu.SMEM)],
        out_specs=vmem,
        scratch_shapes=[
            pltpu.VMEM((blocks, slab, cols), BF16),
            pltpu.VMEM((n, row_t, half), BF16),
            pltpu.VMEM((n, row_t, half), BF16),
            pltpu.VMEM((n, row_t, half), BF16),
            pltpu.VMEM((n, row_t, half), BF16),
            pltpu.VMEM((n, chips - 1, row_t, width), BF16),
            pltpu.VMEM((row_t, width), F32),
            pltpu.VMEM((row_t, width), F32),
            pltpu.VMEM((row_t, width), F32),
            pltpu.VMEM((m, row_t, width), BF16),
            pltpu.VMEM((m, planes - 1, row_t, width), BF16),
            pltpu.VMEM((m, row_t, slab), BF16),
            dma((n,)), dma((n,)),
            dma((n, chips - 1)), dma((n, chips - 1)),
            dma((m, planes - 1)), dma((m, planes - 1)),
            dma((m,)), dma((m, planes - 1)), dma((m, chips)),
            dma((steps, chips - 1)), dma((steps, chips - 1)),
            dma((steps, chips)), dma((steps, chips)),
        ],
        compiler_params=pltpu.CompilerParams(
            collective_id=0, has_side_effects=True, vmem_limit_bytes=48 * 1024 * 1024),
        cost_estimate=pl.CostEstimate(
            flops=2 * blocks * steps * row_t * slab * cols, bytes_accessed=2 * slab * cols, transcendentals=0),
    )(history, self_rows, edge_rows, step_inv, coupling.reshape(1, row_t), reach)


def solution(mesh):
    placed = (P("hist", "second"), P(None, "hist"), P(None, "second"), P(), P(), P())
    return jax.shard_map(
        functools.partial(local, mesh.shape["hist"], mesh.shape["second"]),
        mesh=mesh, in_specs=placed, out_specs=P(None, "second"), check_vma=False
    )
```

```python
import functools

import jax
import jax.numpy as jnp
from jax import lax
from jax.experimental import pallas as pl
from jax.experimental.pallas import tpu as pltpu
from jax.sharding import PartitionSpec as P

MESH = pl.DeviceIdType.MESH
CORES = 2
LANES = 128
BF16 = jnp.bfloat16
F32 = jnp.float32


def kernel(dims, hist_hbm, self_hbm, edge_hbm, inv_hbm, coup_hbm, reach_ref, out_ref,
           hist_ref, self_ref, edge_ref, inv_ref, coup_ref, load_s, masked, psend, pown, arecv, presum, rrecv, acc, green, weights, piece, relay, sig,
           a0_s, a0_r, a1_s, a1_r, z_s, z_r, home_s, fwd_s, sig_r, ag_s, ag_r, mg_s, mg_r):
    chips, planes, owners, width, row_t, steps, blocks, below = dims
    slab, cols = hist_hbm.shape
    half = cols // CORES
    past, tiles = slab // row_t, cols // row_t
    h = lax.axis_index("hist")
    s = lax.axis_index("second")
    q, c = h // CORES, lax.rem(h, CORES)
    mate = q * CORES + 1 - c
    pending = []

    def when(cond, fn):
        if cond is True:
            fn()
        else:
            pl.when(cond)(fn)

    def both(*conds):
        total = True
        for cond in conds:
            if cond is True:
                continue
            total = cond if total is True else jnp.logical_and(total, cond)
        return total

    def owns(chip):
        return True if owners == chips else chip < owners

    def live(hh, plane):
        return hh * past < (plane + 1) * tiles - 1 + 2 * (blocks - 1) + 4

    def remote(src, dst, send, recv, hist_to, second_to):
        return pltpu.make_async_remote_copy(
            src_ref=src, dst_ref=dst, send_sem=send, recv_sem=recv,
            device_id={"hist": hist_to, "second": second_to}, device_id_type=MESH)

    def start(cond, copy):
        when(cond, copy.start)
        pending.append((cond, copy))

    live_me, live_mate = live(h, s), live(mate, s)
    mine = owns(q)

    def half_load(core, n):
        at = pl.ds(pl.multiple_of(core * half, half), half)
        return pltpu.make_async_copy(hist_hbm.at[:, at], hist_ref.at[:, at], load_s.at[n])

    load_first, load_second = half_load(1 - c, 0), half_load(c, 1)
    load_self = pltpu.make_async_copy(self_hbm, self_ref, load_s.at[2])
    edge_at = pl.ds(pl.multiple_of(c * half, half), half)
    load_small = [
        pltpu.make_async_copy(edge_hbm.at[:, edge_at], edge_ref, load_s.at[3]),
        pltpu.make_async_copy(inv_hbm, inv_ref, load_s.at[4]),
        pltpu.make_async_copy(coup_hbm, coup_ref, load_s.at[5]),
    ]
    for load in [load_first, load_self, load_second] + load_small:
        load.start()

    barrier = pltpu.get_barrier_semaphore()

    def greet(hist_to, second_to):
        pl.semaphore_signal(barrier, inc=1, device_id={"hist": hist_to, "second": second_to},
                            device_id_type=MESH)

    greet(mate, s)
    for d in range(1, chips):
        greet(lax.rem(q + d, chips) * CORES + c, s)
    for d in range(1, planes):
        greet(h, lax.rem(s + d, planes))

    def chip_cols(chip):
        return pl.ds(pl.multiple_of(chip * width, width), width)

    def own_cols(chip, core):
        return pl.ds(pl.multiple_of(core * half + chip * width, width), width)

    def make_mask(b, core):
        def work():
            def body(ct, carry):
                tile = core * (tiles // CORES) + ct
                limit = reach_ref[b, s * tiles + tile]
                at = pl.ds(pl.multiple_of(tile * row_t, row_t), row_t)
                for kt in range(past):
                    keep = jnp.where(h * past + kt < limit, 1.0, 0.0).astype(F32)
                    rows = slice(kt * row_t, (kt + 1) * row_t)
                    masked[b, rows, at] = hist_ref[rows, at] * jnp.full((row_t, row_t), keep, F32).astype(BF16)
                return carry
            lax.fori_loop(0, tiles // CORES, body, 0)
        when(live_me, work)

    def product(b, i, dst, core):
        idx = b * steps + i
        chunk = 256

        def body(t, carry):
            left = self_ref[i * row_t:(i + 1) * row_t, :] if b == 0 else sig[idx - steps]
            at = pl.ds(pl.multiple_of(core * half + t * chunk, chunk), chunk)
            to = pl.ds(pl.multiple_of(t * chunk, chunk), chunk)
            dst[idx, :, to] = jnp.dot(left, masked[b, :, at], preferred_element_type=F32).astype(BF16)
            return carry
        lax.fori_loop(0, half // chunk, body, 0)

    def a0_copy(idx):
        return remote(psend.at[idx], arecv.at[idx], a0_s.at[idx], a0_r.at[idx], mate, s)

    def sig_wait(idx):
        for e in range(1, chips):
            p = lax.rem(q + e, chips)

            def wait(p=p):
                spot = sig.at[idx, :, chip_cols(p)]
                remote(spot, spot, home_s.at[idx], sig_r.at[idx, p], p * CORES + c, s).wait_recv()
            when(owns(p), wait)

    def stage_product(b, i):
        idx = b * steps + i

        def first():
            if b:
                sig_wait(idx - steps)
            product(b, i, psend, 1 - c)
        when(live_me, first)
        if idx == 0:
            pl.semaphore_wait(barrier, 1 + (chips - 1) + (planes - 1))
        start(live_me, a0_copy(idx))
        when(live_me, lambda: product(b, i, pown, c))

    def a1_copy(idx, d):
        to = lax.rem(q + d, chips)
        return remote(presum.at[idx, :, chip_cols(to)], rrecv.at[idx, d - 1],
                      a1_s.at[idx, d - 1], a1_r.at[idx, d - 1], to * CORES + c, s)

    def stage_pair(b, i):
        idx = b * steps + i

        def pair():
            a0_copy(idx).wait_recv()
            presum[idx] = (pown[idx].astype(F32) + arecv[idx].astype(F32)).astype(BF16)

        def alone():
            presum[idx] = pown[idx]

        def other():
            a0_copy(idx).wait_recv()
            presum[idx] = arecv[idx]
        no_me, no_mate = jnp.logical_not(live_me), jnp.logical_not(live_mate)
        when(both(live_me, live_mate), pair)
        when(both(live_me, no_mate), alone)
        when(both(no_me, live_mate), other)
        for d in range(1, chips):
            to = lax.rem(q + d, chips)
            start(both(live(q * CORES, s), owns(to)), a1_copy(idx, d))

    def stage_reduce(b, i):
        idx = b * steps + i
        last = b + 1 == blocks

        def init():
            acc[...] = jnp.zeros_like(acc)

        def own():
            acc[...] = presum[idx, :, chip_cols(q)].astype(F32)

        when(mine, init)
        when(both(mine, live(q * CORES, s)), own)
        for d in range(1, chips):
            src = lax.rem(q + chips - d, chips)

            def add(d=d):
                a1_copy(idx, d).wait_recv()
                acc[...] += rrecv[idx, d - 1].astype(F32)
            when(both(mine, live(src * CORES, s)), add)

        def step():
            fresh = jnp.dot(inv_ref[...], green[...] + acc[...], precision=lax.Precision.HIGHEST,
                            preferred_element_type=F32)
            green[...] = fresh
            if last:
                out_ref[i * row_t:(i + 1) * row_t, own_cols(q, c)] = fresh.astype(BF16)
            else:
                square = fresh * fresh
                piece[idx] = (weights[...] * fresh * square / (1.0 + square)).astype(BF16)
        when(mine, step)
        if last:
            rows = slice(i * row_t, (i + 1) * row_t)
            spot = out_ref.at[rows, own_cols(q, c)]
            for d in range(1, chips):
                start(mine, remote(spot, spot, ag_s.at[i, d - 1], ag_r.at[i, d - 1],
                                   lax.rem(q + d, chips) * CORES + c, s))
            start(mine, remote(spot, spot, mg_s.at[i, 0], mg_r.at[i, 0], mate, s))
            return
        start(both(mine, s + 1 < planes), up_copy(idx, 0))
        for e in range(1, below + 1):
            start(both(mine, s >= e, live(s * CORES + c, s - e)), down_copy(idx, e, s - e))
        spot = sig.at[idx, :, chip_cols(q)]
        start(both(mine, q != s), remote(piece.at[idx], spot, home_s.at[idx], sig_r.at[idx, q], s * CORES + c, s))

        def keep():
            sig[idx, :, chip_cols(q)] = piece[idx]
        when(both(mine, q == s), keep)

    def up_copy(idx, d):
        src = piece.at[idx] if d == 0 else relay.at[idx, d - 1]
        return remote(src, relay.at[idx, d], z_s.at[idx, d], z_r.at[idx, d], h, lax.rem(s + 1, planes))

    def down_copy(idx, e, to):
        slot = planes - 2 + e
        return remote(piece.at[idx], relay.at[idx, slot], z_s.at[idx, slot], z_r.at[idx, slot],
                      h, lax.rem(to + planes, planes))

    def pass_on(idx, slot, src, used):
        start(both(used, q != src),
              remote(relay.at[idx, slot], sig.at[idx, :, chip_cols(q)], fwd_s.at[idx, slot], sig_r.at[idx, q],
                     lax.rem(src + planes, planes) * CORES + c, s))

        def keep():
            sig[idx, :, chip_cols(q)] = relay[idx, slot]
        when(both(used, q == src), keep)

    def stage_up(b, i, d):
        idx = b * steps + i
        used = both(mine, s >= d)

        def wait():
            landed = relay.at[idx, d - 1]
            remote(landed, landed, z_s.at[idx, d - 1], z_r.at[idx, d - 1], h, lax.rem(s + planes - 1, planes)).wait_recv()
        when(used, wait)
        if d < planes - 1:
            start(both(used, s + 1 < planes), up_copy(idx, d))
        pass_on(idx, d - 1, s - d, used)

    def stage_down(b, i):
        idx = b * steps + i
        for e in range(1, below + 1):
            used = both(mine, s + e < planes, live((s + e) * CORES + c, s))
            when(used, down_copy(idx, e, s + e).wait_recv)
            pass_on(idx, planes - 2 + e, s + e, used)

    def forward_first(b, i):
        stage_up(b, i, 1)

    def forward_rest(b, i):
        for d in range(2, planes):
            stage_up(b, i, d)
        stage_down(b, i)

    def stage_gather(i):
        rows = slice(i * row_t, (i + 1) * row_t)
        for d in range(1, chips):
            src = lax.rem(q + chips - d, chips)
            spot = out_ref.at[rows, own_cols(src, c)]

            def wait(spot=spot, src=src, d=d):
                remote(spot, spot, ag_s.at[i, d - 1], ag_r.at[i, d - 1], src * CORES + c, s).wait_recv()
            when(owns(src), wait)
            start(owns(src), remote(spot, spot, mg_s.at[i, d], mg_r.at[i, d], mate, s))

    def stage_close(i):
        rows = slice(i * row_t, (i + 1) * row_t)
        for d in range(chips):
            src = lax.rem(q + chips - d, chips)

            def wait(src=src, d=d):
                spot = out_ref.at[rows, own_cols(src, 1 - c)]
                remote(spot, spot, mg_s.at[i, d], mg_r.at[i, d], mate, s).wait_recv()
            when(owns(src), wait)

    load_first.wait()
    load_self.wait()
    make_mask(0, 1 - c)
    load_second.wait()
    make_mask(0, c)
    for b in range(blocks):
        for i in range(steps):
            stage_product(b, i)
        for i in range(steps):
            stage_pair(b, i)
        if b == 0:
            for load in load_small:
                load.wait()
            row = lax.broadcasted_iota(jnp.int32, (row_t, row_t), 0)
            col = lax.broadcasted_iota(jnp.int32, (row_t, row_t), 1)
            spread = jnp.where(row == col, jnp.broadcast_to(coup_ref[...], (row_t, row_t)), 0.0)
            weights[...] = jnp.broadcast_to(jnp.sum(spread, axis=1, keepdims=True), weights.shape)

            def first_green():
                green[...] = edge_ref[:, chip_cols(q)].astype(F32)
            when(mine, first_green)
        if b + 1 < blocks:
            make_mask(b + 1, 0)
            make_mask(b + 1, 1)
        for i in range(steps):
            stage_reduce(b, i)
        for i in range(steps):
            if b + 1 < blocks:
                forward_first(b, i)
                forward_rest(b, i)
            else:
                stage_gather(i)
    for i in range(steps):
        stage_close(i)
    for cond, copy in pending:
        when(cond, copy.wait_send)


def local(hist_count, second_count, history, self_rows, edge_rows, step_inv, coupling, reach):
    slab, cols = history.shape
    row_t = step_inv.shape[0]
    steps = self_rows.shape[0] // row_t
    blocks = reach.shape[0]
    chips, planes = hist_count // CORES, second_count
    half = cols // CORES
    owners = min(chips, half // LANES)
    width = half // owners
    assert chips == planes and half == slab
    past, tiles = slab // row_t, cols // row_t
    below = (tiles + 2 + 2 * (blocks - 1)) // (CORES * past)
    slots = planes - 1 + below
    dims = (chips, planes, owners, width, row_t, steps, blocks, below)
    n, m = blocks * steps, (blocks - 1) * steps
    vmem = pl.BlockSpec(memory_space=pltpu.VMEM)
    dma = pltpu.SemaphoreType.DMA
    return pl.pallas_call(
        functools.partial(kernel, dims),
        out_shape=jax.ShapeDtypeStruct((steps * row_t, cols), BF16),
        in_specs=[pl.BlockSpec(memory_space=pl.ANY)] * 5 + [pl.BlockSpec(memory_space=pltpu.SMEM)],
        out_specs=vmem,
        scratch_shapes=[
            pltpu.VMEM((slab, cols), BF16),
            pltpu.VMEM(self_rows.shape, BF16),
            pltpu.VMEM((row_t, half), BF16),
            pltpu.VMEM((row_t, row_t), F32),
            pltpu.VMEM((1, row_t), F32),
            dma((6,)),
            pltpu.VMEM((blocks, slab, cols), BF16),
            pltpu.VMEM((n, row_t, half), BF16),
            pltpu.VMEM((n, row_t, half), BF16),
            pltpu.VMEM((n, row_t, half), BF16),
            pltpu.VMEM((n, row_t, half), BF16),
            pltpu.VMEM((n, chips - 1, row_t, width), BF16),
            pltpu.VMEM((row_t, width), F32),
            pltpu.VMEM((row_t, width), F32),
            pltpu.VMEM((row_t, width), F32),
            pltpu.VMEM((m, row_t, width), BF16),
            pltpu.VMEM((m, slots, row_t, width), BF16),
            pltpu.VMEM((m, row_t, slab), BF16),
            dma((n,)), dma((n,)),
            dma((n, chips - 1)), dma((n, chips - 1)),
            dma((m, slots)), dma((m, slots)),
            dma((m,)), dma((m, slots)), dma((m, chips)),
            dma((steps, chips - 1)), dma((steps, chips - 1)),
            dma((steps, chips)), dma((steps, chips)),
        ],
        compiler_params=pltpu.CompilerParams(
            collective_id=0, has_side_effects=True, vmem_limit_bytes=56 * 1024 * 1024),
        cost_estimate=pl.CostEstimate(
            flops=2 * blocks * steps * row_t * slab * cols, bytes_accessed=2 * slab * cols, transcendentals=0),
    )(history, self_rows, edge_rows, step_inv, coupling.reshape(1, row_t), reach)


def solution(mesh):
    placed = (P("hist", "second"), P(None, "hist"), P(None, "second"), P(), P(), P())
    return jax.shard_map(
        functools.partial(local, mesh.shape["hist"], mesh.shape["second"]),
        mesh=mesh, in_specs=placed, out_specs=P(None, "second"), check_vma=False
    )
```

```python
import functools

import jax
import jax.numpy as jnp
from jax import lax
from jax.experimental import pallas as pl
from jax.experimental.pallas import tpu as pltpu
from jax.sharding import PartitionSpec as P

MESH = pl.DeviceIdType.MESH
CORES = 2
LANES = 128
BF16 = jnp.bfloat16
F32 = jnp.float32


def kernel(dims, hist_hbm, self_hbm, edge_hbm, inv_hbm, coup_hbm, reach_ref, out_ref,
           hist_ref, self_ref, edge_ref, inv_ref, coup_ref, load_s, masked, psend, pown, arecv, presum, rrecv, acc, green, weights, piece, relay, sig,
           a0_s, a0_r, a1_s, a1_r, z_s, z_r, home_s, fwd_s, sig_r, ag_s, ag_r, mg_s, mg_r):
    chips, planes, owners, width, row_t, steps, blocks, below = dims
    slab, cols = hist_hbm.shape
    half = cols // CORES
    past, tiles = slab // row_t, cols // row_t
    h = lax.axis_index("hist")
    s = lax.axis_index("second")
    q, c = h // CORES, lax.rem(h, CORES)
    mate = q * CORES + 1 - c
    pending = []

    def when(cond, fn):
        if cond is True:
            fn()
        else:
            pl.when(cond)(fn)

    def both(*conds):
        total = True
        for cond in conds:
            if cond is True:
                continue
            total = cond if total is True else jnp.logical_and(total, cond)
        return total

    def owns(chip):
        return True if owners == chips else chip < owners

    def live(hh, plane):
        return hh * past < (plane + 1) * tiles - 1 + 2 * (blocks - 1) + 4

    def remote(src, dst, send, recv, hist_to, second_to):
        return pltpu.make_async_remote_copy(
            src_ref=src, dst_ref=dst, send_sem=send, recv_sem=recv,
            device_id={"hist": hist_to, "second": second_to}, device_id_type=MESH)

    def start(cond, copy):
        when(cond, copy.start)
        pending.append((cond, copy))

    live_me, live_mate = live(h, s), live(mate, s)
    mine = owns(q)

    def half_load(core, n):
        at = pl.ds(pl.multiple_of(core * half, half), half)
        return pltpu.make_async_copy(hist_hbm.at[:, at], hist_ref.at[:, at], load_s.at[n])

    load_first, load_second = half_load(1 - c, 0), half_load(c, 1)
    load_self = pltpu.make_async_copy(self_hbm, self_ref, load_s.at[2])
    edge_at = pl.ds(pl.multiple_of(c * half, half), half)
    load_small = [
        pltpu.make_async_copy(edge_hbm.at[:, edge_at], edge_ref, load_s.at[3]),
        pltpu.make_async_copy(inv_hbm, inv_ref, load_s.at[4]),
        pltpu.make_async_copy(coup_hbm, coup_ref, load_s.at[5]),
    ]
    for load in [load_first, load_self, load_second] + load_small:
        load.start()

    barrier = pltpu.get_barrier_semaphore()

    def greet(hist_to, second_to):
        pl.semaphore_signal(barrier, inc=1, device_id={"hist": hist_to, "second": second_to},
                            device_id_type=MESH)

    greet(mate, s)
    for d in range(1, chips):
        greet(lax.rem(q + d, chips) * CORES + c, s)
    for d in range(1, planes):
        greet(h, lax.rem(s + d, planes))

    def chip_cols(chip):
        return pl.ds(pl.multiple_of(chip * width, width), width)

    def own_cols(chip, core):
        return pl.ds(pl.multiple_of(core * half + chip * width, width), width)

    def make_mask(b, core):
        def work():
            def body(ct, carry):
                tile = core * (tiles // CORES) + ct
                limit = reach_ref[b, s * tiles + tile]
                at = pl.ds(pl.multiple_of(tile * row_t, row_t), row_t)
                for kt in range(past):
                    keep = jnp.where(h * past + kt < limit, 1.0, 0.0).astype(F32)
                    rows = slice(kt * row_t, (kt + 1) * row_t)
                    masked[b, rows, at] = hist_ref[rows, at] * jnp.full((row_t, row_t), keep, F32).astype(BF16)
                return carry
            lax.fori_loop(0, tiles // CORES, body, 0)
        when(live_me, work)

    def product(b, dst, core):
        base = b * steps
        chunk = 256

        def body(t, carry):
            left = self_ref[...] if b == 0 else sig[base - steps:base].reshape(steps * row_t, slab)
            at = pl.ds(pl.multiple_of(core * half + t * chunk, chunk), chunk)
            to = pl.ds(pl.multiple_of(t * chunk, chunk), chunk)
            result = jnp.dot(left, masked[b, :, at], preferred_element_type=F32).astype(BF16)
            for i in range(steps):
                dst[base + i, :, to] = result[i * row_t:(i + 1) * row_t]
            return carry
        lax.fori_loop(0, half // chunk, body, 0)

    def a0_copy(idx):
        return remote(psend.at[idx], arecv.at[idx], a0_s.at[idx], a0_r.at[idx], mate, s)

    def sig_wait(idx):
        for e in range(1, chips):
            p = lax.rem(q + e, chips)

            def wait(p=p):
                spot = sig.at[idx, :, chip_cols(p)]
                remote(spot, spot, home_s.at[idx], sig_r.at[idx, p], p * CORES + c, s).wait_recv()
            when(owns(p), wait)

    def stage_product(b):
        base = b * steps

        def first():
            if b:
                for i in range(steps):
                    sig_wait(base - steps + i)
            product(b, psend, 1 - c)
        when(live_me, first)
        if b == 0:
            pl.semaphore_wait(barrier, 1 + (chips - 1) + (planes - 1))
        for i in range(steps):
            start(live_me, a0_copy(base + i))
        if b == 0:
            load_second.wait()
            make_mask(0, c)
        when(live_me, lambda: product(b, pown, c))

    def a1_copy(idx, d):
        to = lax.rem(q + d, chips)
        return remote(presum.at[idx, :, chip_cols(to)], rrecv.at[idx, d - 1],
                      a1_s.at[idx, d - 1], a1_r.at[idx, d - 1], to * CORES + c, s)

    def stage_pair(b, i):
        idx = b * steps + i

        def pair():
            a0_copy(idx).wait_recv()
            presum[idx] = (pown[idx].astype(F32) + arecv[idx].astype(F32)).astype(BF16)

        def alone():
            presum[idx] = pown[idx]

        def other():
            a0_copy(idx).wait_recv()
            presum[idx] = arecv[idx]
        no_me, no_mate = jnp.logical_not(live_me), jnp.logical_not(live_mate)
        when(both(live_me, live_mate), pair)
        when(both(live_me, no_mate), alone)
        when(both(no_me, live_mate), other)
        for d in range(1, chips):
            to = lax.rem(q + d, chips)
            start(both(live(q * CORES, s), owns(to)), a1_copy(idx, d))

    def stage_reduce(b, i):
        idx = b * steps + i
        last = b + 1 == blocks

        def init():
            acc[...] = jnp.zeros_like(acc)

        def own():
            acc[...] = presum[idx, :, chip_cols(q)].astype(F32)

        when(mine, init)
        when(both(mine, live(q * CORES, s)), own)
        for d in range(1, chips):
            src = lax.rem(q + chips - d, chips)

            def add(d=d):
                a1_copy(idx, d).wait_recv()
                acc[...] += rrecv[idx, d - 1].astype(F32)
            when(both(mine, live(src * CORES, s)), add)

        def step():
            fresh = jnp.dot(inv_ref[...], green[...] + acc[...], precision=lax.Precision.HIGHEST,
                            preferred_element_type=F32)
            green[...] = fresh
            if last:
                out_ref[i * row_t:(i + 1) * row_t, own_cols(q, c)] = fresh.astype(BF16)
            else:
                square = fresh * fresh
                piece[idx] = (weights[...] * fresh * square / (1.0 + square)).astype(BF16)
        when(mine, step)
        if last:
            rows = slice(i * row_t, (i + 1) * row_t)
            spot = out_ref.at[rows, own_cols(q, c)]
            for d in range(1, chips):
                start(mine, remote(spot, spot, ag_s.at[i, d - 1], ag_r.at[i, d - 1],
                                   lax.rem(q + d, chips) * CORES + c, s))
            start(mine, remote(spot, spot, mg_s.at[i, 0], mg_r.at[i, 0], mate, s))
            return
        start(both(mine, s + 1 < planes), up_copy(idx, 0))
        for e in range(1, below + 1):
            start(both(mine, s >= e, live(s * CORES + c, s - e)), down_copy(idx, e, s - e))
        spot = sig.at[idx, :, chip_cols(q)]
        start(both(mine, q != s), remote(piece.at[idx], spot, home_s.at[idx], sig_r.at[idx, q], s * CORES + c, s))

        def keep():
            sig[idx, :, chip_cols(q)] = piece[idx]
        when(both(mine, q == s), keep)

    def up_copy(idx, d):
        src = piece.at[idx] if d == 0 else relay.at[idx, d - 1]
        return remote(src, relay.at[idx, d], z_s.at[idx, d], z_r.at[idx, d], h, lax.rem(s + 1, planes))

    def down_copy(idx, e, to):
        slot = planes - 2 + e
        return remote(piece.at[idx], relay.at[idx, slot], z_s.at[idx, slot], z_r.at[idx, slot],
                      h, lax.rem(to + planes, planes))

    def pass_on(idx, slot, src, used):
        start(both(used, q != src),
              remote(relay.at[idx, slot], sig.at[idx, :, chip_cols(q)], fwd_s.at[idx, slot], sig_r.at[idx, q],
                     lax.rem(src + planes, planes) * CORES + c, s))

        def keep():
            sig[idx, :, chip_cols(q)] = relay[idx, slot]
        when(both(used, q == src), keep)

    def stage_up(b, i, d):
        idx = b * steps + i
        used = both(mine, s >= d)

        def wait():
            landed = relay.at[idx, d - 1]
            remote(landed, landed, z_s.at[idx, d - 1], z_r.at[idx, d - 1], h, lax.rem(s + planes - 1, planes)).wait_recv()
        when(used, wait)
        if d < planes - 1:
            start(both(used, s + 1 < planes), up_copy(idx, d))
        pass_on(idx, d - 1, s - d, used)

    def stage_down(b, i):
        idx = b * steps + i
        for e in range(1, below + 1):
            used = both(mine, s + e < planes, live((s + e) * CORES + c, s))
            when(used, down_copy(idx, e, s + e).wait_recv)
            pass_on(idx, planes - 2 + e, s + e, used)

    def forward_first(b, i):
        stage_up(b, i, 1)

    def forward_rest(b, i):
        for d in range(2, planes):
            stage_up(b, i, d)
        stage_down(b, i)

    def stage_gather(i):
        rows = slice(i * row_t, (i + 1) * row_t)
        for d in range(1, chips):
            src = lax.rem(q + chips - d, chips)
            spot = out_ref.at[rows, own_cols(src, c)]

            def wait(spot=spot, src=src, d=d):
                remote(spot, spot, ag_s.at[i, d - 1], ag_r.at[i, d - 1], src * CORES + c, s).wait_recv()
            when(owns(src), wait)
            start(owns(src), remote(spot, spot, mg_s.at[i, d], mg_r.at[i, d], mate, s))

    def stage_close(i):
        rows = slice(i * row_t, (i + 1) * row_t)
        for d in range(chips):
            src = lax.rem(q + chips - d, chips)

            def wait(src=src, d=d):
                spot = out_ref.at[rows, own_cols(src, 1 - c)]
                remote(spot, spot, mg_s.at[i, d], mg_r.at[i, d], mate, s).wait_recv()
            when(owns(src), wait)

    load_first.wait()
    load_self.wait()
    make_mask(0, 1 - c)
    for b in range(blocks):
        stage_product(b)
        for i in range(steps):
            stage_pair(b, i)
        if b == 0:
            for load in load_small:
                load.wait()
            row = lax.broadcasted_iota(jnp.int32, (row_t, row_t), 0)
            col = lax.broadcasted_iota(jnp.int32, (row_t, row_t), 1)
            spread = jnp.where(row == col, jnp.broadcast_to(coup_ref[...], (row_t, row_t)), 0.0)
            weights[...] = jnp.broadcast_to(jnp.sum(spread, axis=1, keepdims=True), weights.shape)

            def first_green():
                green[...] = edge_ref[:, chip_cols(q)].astype(F32)
            when(mine, first_green)
        if b + 1 < blocks:
            make_mask(b + 1, 0)
            make_mask(b + 1, 1)
        for i in range(steps):
            stage_reduce(b, i)
        for i in range(steps):
            if b + 1 < blocks:
                forward_first(b, i)
                forward_rest(b, i)
            else:
                stage_gather(i)
    for i in range(steps):
        stage_close(i)
    for cond, copy in pending:
        when(cond, copy.wait_send)


def local(hist_count, second_count, history, self_rows, edge_rows, step_inv, coupling, reach):
    slab, cols = history.shape
    row_t = step_inv.shape[0]
    steps = self_rows.shape[0] // row_t
    blocks = reach.shape[0]
    chips, planes = hist_count // CORES, second_count
    half = cols // CORES
    owners = min(chips, half // LANES)
    width = half // owners
    assert chips == planes and half == slab
    past, tiles = slab // row_t, cols // row_t
    below = (tiles + 2 + 2 * (blocks - 1)) // (CORES * past)
    slots = planes - 1 + below
    dims = (chips, planes, owners, width, row_t, steps, blocks, below)
    n, m = blocks * steps, (blocks - 1) * steps
    vmem = pl.BlockSpec(memory_space=pltpu.VMEM)
    dma = pltpu.SemaphoreType.DMA
    return pl.pallas_call(
        functools.partial(kernel, dims),
        out_shape=jax.ShapeDtypeStruct((steps * row_t, cols), BF16),
        in_specs=[pl.BlockSpec(memory_space=pl.ANY)] * 5 + [pl.BlockSpec(memory_space=pltpu.SMEM)],
        out_specs=vmem,
        scratch_shapes=[
            pltpu.VMEM((slab, cols), BF16),
            pltpu.VMEM(self_rows.shape, BF16),
            pltpu.VMEM((row_t, half), BF16),
            pltpu.VMEM((row_t, row_t), F32),
            pltpu.VMEM((1, row_t), F32),
            dma((6,)),
            pltpu.VMEM((blocks, slab, cols), BF16),
            pltpu.VMEM((n, row_t, half), BF16),
            pltpu.VMEM((n, row_t, half), BF16),
            pltpu.VMEM((n, row_t, half), BF16),
            pltpu.VMEM((n, row_t, half), BF16),
            pltpu.VMEM((n, chips - 1, row_t, width), BF16),
            pltpu.VMEM((row_t, width), F32),
            pltpu.VMEM((row_t, width), F32),
            pltpu.VMEM((row_t, width), F32),
            pltpu.VMEM((m, row_t, width), BF16),
            pltpu.VMEM((m, slots, row_t, width), BF16),
            pltpu.VMEM((m, row_t, slab), BF16),
            dma((n,)), dma((n,)),
            dma((n, chips - 1)), dma((n, chips - 1)),
            dma((m, slots)), dma((m, slots)),
            dma((m,)), dma((m, slots)), dma((m, chips)),
            dma((steps, chips - 1)), dma((steps, chips - 1)),
            dma((steps, chips)), dma((steps, chips)),
        ],
        compiler_params=pltpu.CompilerParams(
            collective_id=0, has_side_effects=True, vmem_limit_bytes=56 * 1024 * 1024),
        cost_estimate=pl.CostEstimate(
            flops=2 * blocks * steps * row_t * slab * cols, bytes_accessed=2 * slab * cols, transcendentals=0),
    )(history, self_rows, edge_rows, step_inv, coupling.reshape(1, row_t), reach)


def solution(mesh):
    placed = (P("hist", "second"), P(None, "hist"), P(None, "second"), P(), P(), P())
    return jax.shard_map(
        functools.partial(local, mesh.shape["hist"], mesh.shape["second"]),
        mesh=mesh, in_specs=placed, out_specs=P(None, "second"), check_vma=False
    )
```

```python
import functools

import jax
import jax.numpy as jnp
from jax import lax
from jax.experimental import pallas as pl
from jax.experimental.pallas import tpu as pltpu
from jax.sharding import PartitionSpec as P

MESH = pl.DeviceIdType.MESH
CORES = 2
LANES = 128
BF16 = jnp.bfloat16
F32 = jnp.float32


def kernel(dims, hist_hbm, self_hbm, edge_hbm, inv_hbm, coup_hbm, reach_ref, out_ref,
           hist_ref, self_ref, edge_ref, inv_ref, coup_ref, load_s, masked, psend, pown, arecv, presum, rrecv, acc, green, weights, piece, relay, sig,
           a0_s, a0_r, a1_s, a1_r, z_s, z_r, home_s, fwd_s, sig_r, ag_s, ag_r, mg_s, mg_r):
    chips, planes, owners, width, row_t, steps, blocks, below = dims
    slab, cols = hist_hbm.shape
    half = cols // CORES
    past, tiles = slab // row_t, cols // row_t
    h = lax.axis_index("hist")
    s = lax.axis_index("second")
    q, c = h // CORES, lax.rem(h, CORES)
    mate = q * CORES + 1 - c
    pending = []

    def when(cond, fn):
        if cond is True:
            fn()
        else:
            pl.when(cond)(fn)

    def both(*conds):
        total = True
        for cond in conds:
            if cond is True:
                continue
            total = cond if total is True else jnp.logical_and(total, cond)
        return total

    def owns(chip):
        return True if owners == chips else chip < owners

    def live(hh, plane):
        return hh * past < (plane + 1) * tiles - 1 + 2 * (blocks - 1) + 4

    def remote(src, dst, send, recv, hist_to, second_to):
        return pltpu.make_async_remote_copy(
            src_ref=src, dst_ref=dst, send_sem=send, recv_sem=recv,
            device_id={"hist": hist_to, "second": second_to}, device_id_type=MESH)

    def start(cond, copy):
        when(cond, copy.start)
        pending.append((cond, copy))

    live_me, live_mate = live(h, s), live(mate, s)
    mine = owns(q)

    def half_load(core, n):
        at = pl.ds(pl.multiple_of(core * half, half), half)
        return pltpu.make_async_copy(hist_hbm.at[:, at], hist_ref.at[:, at], load_s.at[n])

    load_first, load_second = half_load(1 - c, 0), half_load(c, 1)
    load_self = pltpu.make_async_copy(self_hbm, self_ref, load_s.at[2])
    edge_at = pl.ds(pl.multiple_of(c * half, half), half)
    load_small = [
        pltpu.make_async_copy(edge_hbm.at[:, edge_at], edge_ref, load_s.at[3]),
        pltpu.make_async_copy(inv_hbm, inv_ref, load_s.at[4]),
        pltpu.make_async_copy(coup_hbm, coup_ref, load_s.at[5]),
    ]
    for load in [load_first, load_self, load_second] + load_small:
        load.start()

    barrier = pltpu.get_barrier_semaphore()

    def greet(hist_to, second_to):
        pl.semaphore_signal(barrier, inc=1, device_id={"hist": hist_to, "second": second_to},
                            device_id_type=MESH)

    greet(mate, s)
    for d in range(1, chips):
        greet(lax.rem(q + d, chips) * CORES + c, s)
    for d in range(1, planes):
        greet(h, lax.rem(s + d, planes))

    def chip_cols(chip):
        return pl.ds(pl.multiple_of(chip * width, width), width)

    def own_cols(chip, core):
        return pl.ds(pl.multiple_of(core * half + chip * width, width), width)

    def make_mask(b, core):
        def work():
            def body(ct, carry):
                tile = core * (tiles // CORES) + ct
                limit = reach_ref[b, s * tiles + tile]
                at = pl.ds(pl.multiple_of(tile * row_t, row_t), row_t)
                for kt in range(past):
                    keep = jnp.where(h * past + kt < limit, 1.0, 0.0).astype(F32)
                    rows = slice(kt * row_t, (kt + 1) * row_t)
                    masked[b, rows, at] = hist_ref[rows, at] * jnp.full((row_t, row_t), keep, F32).astype(BF16)
                return carry
            lax.fori_loop(0, tiles // CORES, body, 0)
        when(live_me, work)

    def product(b, dst, core):
        base = b * steps
        chunk = 256

        def body(t, carry):
            left = self_ref[...] if b == 0 else sig[base - steps:base].reshape(steps * row_t, slab)
            at = pl.ds(pl.multiple_of(core * half + t * chunk, chunk), chunk)
            to = pl.ds(pl.multiple_of(t * chunk, chunk), chunk)
            result = jnp.dot(left, masked[b, :, at], preferred_element_type=F32).astype(BF16)
            for i in range(steps):
                dst[base + i, :, to] = result[i * row_t:(i + 1) * row_t]
            return carry
        lax.fori_loop(0, half // chunk, body, 0)

    def a0_copy(idx):
        return remote(psend.at[idx], arecv.at[idx], a0_s.at[idx], a0_r.at[idx], mate, s)

    def sig_wait(idx):
        for e in range(1, chips):
            p = lax.rem(q + e, chips)

            def wait(p=p):
                spot = sig.at[idx, :, chip_cols(p)]
                remote(spot, spot, home_s.at[idx], sig_r.at[idx, p], p * CORES + c, s).wait_recv()
            when(owns(p), wait)

    def stage_product(b):
        base = b * steps

        def first():
            if b:
                for i in range(steps):
                    sig_wait(base - steps + i)
            product(b, psend, 1 - c)
        when(live_me, first)
        if b == 0:
            pl.semaphore_wait(barrier, 1 + (chips - 1) + (planes - 1))
        for i in range(steps):
            start(live_me, a0_copy(base + i))
        if b == 0:
            load_second.wait()
            make_mask(0, c)
        when(live_me, lambda: product(b, pown, c))

    def a1_copy(idx, d):
        to = lax.rem(q + d, chips)
        return remote(presum.at[idx, :, chip_cols(to)], rrecv.at[idx, d - 1],
                      a1_s.at[idx, d - 1], a1_r.at[idx, d - 1], to * CORES + c, s)

    def stage_pair(b, i):
        idx = b * steps + i

        def pair():
            a0_copy(idx).wait_recv()
            presum[idx] = (pown[idx].astype(F32) + arecv[idx].astype(F32)).astype(BF16)

        def alone():
            presum[idx] = pown[idx]

        def other():
            a0_copy(idx).wait_recv()
            presum[idx] = arecv[idx]
        no_me, no_mate = jnp.logical_not(live_me), jnp.logical_not(live_mate)
        when(both(live_me, live_mate), pair)
        when(both(live_me, no_mate), alone)
        when(both(no_me, live_mate), other)
        for d in range(1, chips):
            to = lax.rem(q + d, chips)
            start(both(live(q * CORES, s), owns(to)), a1_copy(idx, d))

    def stage_reduce(b, i):
        idx = b * steps + i
        last = b + 1 == blocks

        def init():
            acc[...] = jnp.zeros_like(acc)

        def own():
            acc[...] = presum[idx, :, chip_cols(q)].astype(F32)

        when(mine, init)
        when(both(mine, live(q * CORES, s)), own)
        for d in range(1, chips):
            src = lax.rem(q + chips - d, chips)

            def add(d=d):
                a1_copy(idx, d).wait_recv()
                acc[...] += rrecv[idx, d - 1].astype(F32)
            when(both(mine, live(src * CORES, s)), add)

        def step():
            fresh = jnp.dot(inv_ref[...], green[...] + acc[...], precision=lax.Precision.HIGHEST,
                            preferred_element_type=F32)
            green[...] = fresh
            if last:
                out_ref[i * row_t:(i + 1) * row_t, own_cols(q, c)] = fresh.astype(BF16)
            else:
                square = fresh * fresh
                piece[idx] = (weights[...] * fresh * square / (1.0 + square)).astype(BF16)
        when(mine, step)
        if last:
            rows = slice(i * row_t, (i + 1) * row_t)
            spot = out_ref.at[rows, own_cols(q, c)]
            for d in range(1, chips):
                start(mine, remote(spot, spot, ag_s.at[i, d - 1], ag_r.at[i, d - 1],
                                   lax.rem(q + d, chips) * CORES + c, s))
            start(mine, remote(spot, spot, mg_s.at[i, 0], mg_r.at[i, 0], mate, s))
            return
        start(both(mine, s + 1 < planes), up_copy(idx, 0))
        for e in range(1, below + 1):
            start(both(mine, s >= e, live(s * CORES + c, s - e)), down_copy(idx, e, s - e))
        spot = sig.at[idx, :, chip_cols(q)]
        start(both(mine, q != s), remote(piece.at[idx], spot, home_s.at[idx], sig_r.at[idx, q], s * CORES + c, s))

        def keep():
            sig[idx, :, chip_cols(q)] = piece[idx]
        when(both(mine, q == s), keep)

    def up_copy(idx, d):
        src = piece.at[idx] if d == 0 else relay.at[idx, d - 1]
        return remote(src, relay.at[idx, d], z_s.at[idx, d], z_r.at[idx, d], h, lax.rem(s + 1, planes))

    def down_copy(idx, e, to):
        slot = planes - 2 + e
        return remote(piece.at[idx], relay.at[idx, slot], z_s.at[idx, slot], z_r.at[idx, slot],
                      h, lax.rem(to + planes, planes))

    def pass_on(idx, slot, src, used):
        start(both(used, q != src),
              remote(relay.at[idx, slot], sig.at[idx, :, chip_cols(q)], fwd_s.at[idx, slot], sig_r.at[idx, q],
                     lax.rem(src + planes, planes) * CORES + c, s))

        def keep():
            sig[idx, :, chip_cols(q)] = relay[idx, slot]
        when(both(used, q == src), keep)

    def stage_up(b, i, d):
        idx = b * steps + i
        used = both(mine, s >= d)

        def wait():
            landed = relay.at[idx, d - 1]
            remote(landed, landed, z_s.at[idx, d - 1], z_r.at[idx, d - 1], h, lax.rem(s + planes - 1, planes)).wait_recv()
        when(used, wait)
        if d < planes - 1:
            start(both(used, s + 1 < planes), up_copy(idx, d))
        pass_on(idx, d - 1, s - d, used)

    def stage_down(b, i):
        idx = b * steps + i
        for e in range(1, below + 1):
            used = both(mine, s + e < planes, live((s + e) * CORES + c, s))
            when(used, down_copy(idx, e, s + e).wait_recv)
            pass_on(idx, planes - 2 + e, s + e, used)

    def stage_gather(i):
        rows = slice(i * row_t, (i + 1) * row_t)
        for d in range(1, chips):
            src = lax.rem(q + chips - d, chips)
            spot = out_ref.at[rows, own_cols(src, c)]

            def wait(spot=spot, src=src, d=d):
                remote(spot, spot, ag_s.at[i, d - 1], ag_r.at[i, d - 1], src * CORES + c, s).wait_recv()
            when(owns(src), wait)
            start(owns(src), remote(spot, spot, mg_s.at[i, d], mg_r.at[i, d], mate, s))

    def stage_close(i):
        rows = slice(i * row_t, (i + 1) * row_t)
        for d in range(chips):
            src = lax.rem(q + chips - d, chips)

            def wait(src=src, d=d):
                spot = out_ref.at[rows, own_cols(src, 1 - c)]
                remote(spot, spot, mg_s.at[i, d], mg_r.at[i, d], mate, s).wait_recv()
            when(owns(src), wait)

    load_first.wait()
    load_self.wait()
    make_mask(0, 1 - c)
    for b in range(blocks):
        stage_product(b)
        for i in range(steps):
            stage_pair(b, i)
        if b == 0:
            for load in load_small:
                load.wait()
            row = lax.broadcasted_iota(jnp.int32, (row_t, row_t), 0)
            col = lax.broadcasted_iota(jnp.int32, (row_t, row_t), 1)
            spread = jnp.where(row == col, jnp.broadcast_to(coup_ref[...], (row_t, row_t)), 0.0)
            weights[...] = jnp.broadcast_to(jnp.sum(spread, axis=1, keepdims=True), weights.shape)

            def first_green():
                green[...] = edge_ref[:, chip_cols(q)].astype(F32)
            when(mine, first_green)
        if b + 1 < blocks:
            make_mask(b + 1, 0)
            make_mask(b + 1, 1)
        for i in range(steps):
            stage_reduce(b, i)
        if b + 1 < blocks:
            for d in range(1, planes):
                for i in range(steps):
                    stage_up(b, i, d)
            for i in range(steps):
                stage_down(b, i)
        else:
            for i in range(steps):
                stage_gather(i)
    for i in range(steps):
        stage_close(i)
    for cond, copy in pending:
        when(cond, copy.wait_send)


def local(hist_count, second_count, history, self_rows, edge_rows, step_inv, coupling, reach):
    slab, cols = history.shape
    row_t = step_inv.shape[0]
    steps = self_rows.shape[0] // row_t
    blocks = reach.shape[0]
    chips, planes = hist_count // CORES, second_count
    half = cols // CORES
    owners = min(chips, half // LANES)
    width = half // owners
    assert chips == planes and half == slab
    past, tiles = slab // row_t, cols // row_t
    below = (tiles + 2 + 2 * (blocks - 1)) // (CORES * past)
    slots = planes - 1 + below
    dims = (chips, planes, owners, width, row_t, steps, blocks, below)
    n, m = blocks * steps, (blocks - 1) * steps
    vmem = pl.BlockSpec(memory_space=pltpu.VMEM)
    dma = pltpu.SemaphoreType.DMA
    return pl.pallas_call(
        functools.partial(kernel, dims),
        out_shape=jax.ShapeDtypeStruct((steps * row_t, cols), BF16),
        in_specs=[pl.BlockSpec(memory_space=pl.ANY)] * 5 + [pl.BlockSpec(memory_space=pltpu.SMEM)],
        out_specs=vmem,
        scratch_shapes=[
            pltpu.VMEM((slab, cols), BF16),
            pltpu.VMEM(self_rows.shape, BF16),
            pltpu.VMEM((row_t, half), BF16),
            pltpu.VMEM((row_t, row_t), F32),
            pltpu.VMEM((1, row_t), F32),
            dma((6,)),
            pltpu.VMEM((blocks, slab, cols), BF16),
            pltpu.VMEM((n, row_t, half), BF16),
            pltpu.VMEM((n, row_t, half), BF16),
            pltpu.VMEM((n, row_t, half), BF16),
            pltpu.VMEM((n, row_t, half), BF16),
            pltpu.VMEM((n, chips - 1, row_t, width), BF16),
            pltpu.VMEM((row_t, width), F32),
            pltpu.VMEM((row_t, width), F32),
            pltpu.VMEM((row_t, width), F32),
            pltpu.VMEM((m, row_t, width), BF16),
            pltpu.VMEM((m, slots, row_t, width), BF16),
            pltpu.VMEM((m, row_t, slab), BF16),
            dma((n,)), dma((n,)),
            dma((n, chips - 1)), dma((n, chips - 1)),
            dma((m, slots)), dma((m, slots)),
            dma((m,)), dma((m, slots)), dma((m, chips)),
            dma((steps, chips - 1)), dma((steps, chips - 1)),
            dma((steps, chips)), dma((steps, chips)),
        ],
        compiler_params=pltpu.CompilerParams(
            collective_id=0, has_side_effects=True, vmem_limit_bytes=56 * 1024 * 1024),
        cost_estimate=pl.CostEstimate(
            flops=2 * blocks * steps * row_t * slab * cols, bytes_accessed=2 * slab * cols, transcendentals=0),
    )(history, self_rows, edge_rows, step_inv, coupling.reshape(1, row_t), reach)


def solution(mesh):
    placed = (P("hist", "second"), P(None, "hist"), P(None, "second"), P(), P(), P())
    return jax.shard_map(
        functools.partial(local, mesh.shape["hist"], mesh.shape["second"]),
        mesh=mesh, in_specs=placed, out_specs=P(None, "second"), check_vma=False
    )
```

```python
import functools

import jax
import jax.numpy as jnp
from jax import lax
from jax.experimental import pallas as pl
from jax.experimental.pallas import tpu as pltpu
from jax.sharding import PartitionSpec as P

MESH = pl.DeviceIdType.MESH
CORES = 2
LANES = 128
BF16 = jnp.bfloat16
F32 = jnp.float32


def kernel(dims, hist_hbm, self_hbm, edge_hbm, inv_hbm, coup_hbm, reach_ref, out_ref,
           hist_ref, self_ref, edge_ref, inv_ref, coup_ref, load_s, masked, psend, pown, arecv, presum, rrecv, acc, green, weights, piece, relay, sig,
           a0_s, a0_r, a1_s, a1_r, z_s, z_r, home_s, fwd_s, sig_r, ag_s, ag_r, mg_s, mg_r):
    chips, planes, owners, width, row_t, steps, blocks, below = dims
    slab, cols = hist_hbm.shape
    half = cols // CORES
    past, tiles = slab // row_t, cols // row_t
    h = lax.axis_index("hist")
    s = lax.axis_index("second")
    q, c = h // CORES, lax.rem(h, CORES)
    mate = q * CORES + 1 - c
    pending = []

    def when(cond, fn):
        if cond is True:
            fn()
        else:
            pl.when(cond)(fn)

    def both(*conds):
        total = True
        for cond in conds:
            if cond is True:
                continue
            total = cond if total is True else jnp.logical_and(total, cond)
        return total

    def owns(chip):
        return True if owners == chips else chip < owners

    def live(hh, plane):
        return hh * past < (plane + 1) * tiles - 1 + 2 * (blocks - 1) + 4

    def remote(src, dst, send, recv, hist_to, second_to):
        return pltpu.make_async_remote_copy(
            src_ref=src, dst_ref=dst, send_sem=send, recv_sem=recv,
            device_id={"hist": hist_to, "second": second_to}, device_id_type=MESH)

    def start(cond, copy):
        when(cond, copy.start)
        pending.append((cond, copy))

    live_me, live_mate = live(h, s), live(mate, s)
    mine = owns(q)

    def half_load(core, n):
        at = pl.ds(pl.multiple_of(core * half, half), half)
        return pltpu.make_async_copy(hist_hbm.at[:, at], hist_ref.at[:, at], load_s.at[n])

    load_first, load_second = half_load(1 - c, 0), half_load(c, 1)
    load_self = pltpu.make_async_copy(self_hbm, self_ref, load_s.at[2])
    edge_at = pl.ds(pl.multiple_of(c * half, half), half)
    load_small = [
        pltpu.make_async_copy(edge_hbm.at[:, edge_at], edge_ref, load_s.at[3]),
        pltpu.make_async_copy(inv_hbm, inv_ref, load_s.at[4]),
        pltpu.make_async_copy(coup_hbm, coup_ref, load_s.at[5]),
    ]
    for load in [load_first, load_self, load_second] + load_small:
        load.start()

    barrier = pltpu.get_barrier_semaphore()

    def greet(hist_to, second_to):
        pl.semaphore_signal(barrier, inc=1, device_id={"hist": hist_to, "second": second_to},
                            device_id_type=MESH)

    greet(mate, s)
    for d in range(1, chips):
        greet(lax.rem(q + d, chips) * CORES + c, s)
    for d in range(1, planes):
        greet(h, lax.rem(s + d, planes))

    def chip_cols(chip):
        return pl.ds(pl.multiple_of(chip * width, width), width)

    def own_cols(chip, core):
        return pl.ds(pl.multiple_of(core * half + chip * width, width), width)

    def make_mask(b, core):
        def work():
            def body(ct, carry):
                tile = core * (tiles // CORES) + ct
                limit = reach_ref[b, s * tiles + tile]
                at = pl.ds(pl.multiple_of(tile * row_t, row_t), row_t)
                for kt in range(past):
                    keep = jnp.where(h * past + kt < limit, 1.0, 0.0).astype(F32)
                    rows = slice(kt * row_t, (kt + 1) * row_t)
                    masked[b, rows, at] = hist_ref[rows, at] * jnp.full((row_t, row_t), keep, F32).astype(BF16)
                return carry
            lax.fori_loop(0, tiles // CORES, body, 0)
        when(live_me, work)

    def product(b, i, dst, core):
        idx = b * steps + i
        chunk = 256

        def body(t, carry):
            left = self_ref[i * row_t:(i + 1) * row_t, :] if b == 0 else sig[idx - steps]
            at = pl.ds(pl.multiple_of(core * half + t * chunk, chunk), chunk)
            to = pl.ds(pl.multiple_of(t * chunk, chunk), chunk)
            dst[idx, :, to] = jnp.dot(left, masked[b, :, at], preferred_element_type=F32).astype(BF16)
            return carry
        lax.fori_loop(0, half // chunk, body, 0)

    def a0_copy(idx):
        return remote(psend.at[idx], arecv.at[idx], a0_s.at[idx], a0_r.at[idx], mate, s)

    def sig_wait(idx):
        for e in range(1, chips):
            p = lax.rem(q + e, chips)

            def wait(p=p):
                spot = sig.at[idx, :, chip_cols(p)]
                remote(spot, spot, home_s.at[idx], sig_r.at[idx, p], p * CORES + c, s).wait_recv()
            when(owns(p), wait)

    def stage_product(b, i):
        idx = b * steps + i

        def first():
            if b:
                sig_wait(idx - steps)
            product(b, i, psend, 1 - c)
        when(live_me, first)
        if idx == 0:
            pl.semaphore_wait(barrier, 1 + (chips - 1) + (planes - 1))
        start(live_me, a0_copy(idx))
        when(live_me, lambda: product(b, i, pown, c))

    def a1_copy(idx, d):
        to = lax.rem(q + d, chips)
        return remote(presum.at[idx, :, chip_cols(to)], rrecv.at[idx, d - 1],
                      a1_s.at[idx, d - 1], a1_r.at[idx, d - 1], to * CORES + c, s)

    def stage_pair(b, i):
        idx = b * steps + i

        def pair():
            a0_copy(idx).wait_recv()
            presum[idx] = (pown[idx].astype(F32) + arecv[idx].astype(F32)).astype(BF16)

        def alone():
            presum[idx] = pown[idx]

        def other():
            a0_copy(idx).wait_recv()
            presum[idx] = arecv[idx]
        no_me, no_mate = jnp.logical_not(live_me), jnp.logical_not(live_mate)
        when(both(live_me, live_mate), pair)
        when(both(live_me, no_mate), alone)
        when(both(no_me, live_mate), other)
        for d in range(1, chips):
            to = lax.rem(q + d, chips)
            start(both(live(q * CORES, s), owns(to)), a1_copy(idx, d))

    def stage_reduce(b, i):
        idx = b * steps + i
        last = b + 1 == blocks

        def init():
            acc[...] = jnp.zeros_like(acc)

        def own():
            acc[...] = presum[idx, :, chip_cols(q)].astype(F32)

        when(mine, init)
        when(both(mine, live(q * CORES, s)), own)
        for d in range(1, chips):
            src = lax.rem(q + chips - d, chips)

            def add(d=d):
                a1_copy(idx, d).wait_recv()
                acc[...] += rrecv[idx, d - 1].astype(F32)
            when(both(mine, live(src * CORES, s)), add)

        def step():
            fresh = jnp.dot(inv_ref[...], green[...] + acc[...], precision=lax.Precision.HIGHEST,
                            preferred_element_type=F32)
            green[...] = fresh
            if last:
                out_ref[i * row_t:(i + 1) * row_t, own_cols(q, c)] = fresh.astype(BF16)
            else:
                square = fresh * fresh
                piece[idx] = (weights[...] * fresh * square / (1.0 + square)).astype(BF16)
        when(mine, step)
        if last:
            rows = slice(i * row_t, (i + 1) * row_t)
            spot = out_ref.at[rows, own_cols(q, c)]
            for d in range(1, chips):
                start(mine, remote(spot, spot, ag_s.at[i, d - 1], ag_r.at[i, d - 1],
                                   lax.rem(q + d, chips) * CORES + c, s))
            start(mine, remote(spot, spot, mg_s.at[i, 0], mg_r.at[i, 0], mate, s))
            return
        start(both(mine, s + 1 < planes), up_copy(idx, 0))
        for e in range(1, below + 1):
            start(both(mine, s >= e, live(s * CORES + c, s - e)), down_copy(idx, e, s - e))
        spot = sig.at[idx, :, chip_cols(q)]
        start(both(mine, q != s), remote(piece.at[idx], spot, home_s.at[idx], sig_r.at[idx, q], s * CORES + c, s))

        def keep():
            sig[idx, :, chip_cols(q)] = piece[idx]
        when(both(mine, q == s), keep)

    def up_copy(idx, d):
        src = piece.at[idx] if d == 0 else relay.at[idx, d - 1]
        return remote(src, relay.at[idx, d], z_s.at[idx, d], z_r.at[idx, d], h, lax.rem(s + 1, planes))

    def down_copy(idx, e, to):
        slot = planes - 2 + e
        return remote(piece.at[idx], relay.at[idx, slot], z_s.at[idx, slot], z_r.at[idx, slot],
                      h, lax.rem(to + planes, planes))

    def pass_on(idx, slot, src, used):
        start(both(used, q != src),
              remote(relay.at[idx, slot], sig.at[idx, :, chip_cols(q)], fwd_s.at[idx, slot], sig_r.at[idx, q],
                     lax.rem(src + planes, planes) * CORES + c, s))

        def keep():
            sig[idx, :, chip_cols(q)] = relay[idx, slot]
        when(both(used, q == src), keep)

    def stage_up(b, i, d):
        idx = b * steps + i
        used = both(mine, s >= d)

        def wait():
            landed = relay.at[idx, d - 1]
            remote(landed, landed, z_s.at[idx, d - 1], z_r.at[idx, d - 1], h, lax.rem(s + planes - 1, planes)).wait_recv()
        when(used, wait)
        if d < planes - 1:
            start(both(used, s + 1 < planes), up_copy(idx, d))
        pass_on(idx, d - 1, s - d, used)

    def stage_down(b, i):
        idx = b * steps + i
        for e in range(1, below + 1):
            used = both(mine, s + e < planes, live((s + e) * CORES + c, s))
            when(used, down_copy(idx, e, s + e).wait_recv)
            pass_on(idx, planes - 2 + e, s + e, used)

    def forward_first(b, i):
        stage_up(b, i, 1)

    def forward_rest(b, i):
        for d in range(2, planes):
            stage_up(b, i, d)
        stage_down(b, i)

    def stage_gather(i):
        rows = slice(i * row_t, (i + 1) * row_t)
        for d in range(1, chips):
            src = lax.rem(q + chips - d, chips)
            spot = out_ref.at[rows, own_cols(src, c)]

            def wait(spot=spot, src=src, d=d):
                remote(spot, spot, ag_s.at[i, d - 1], ag_r.at[i, d - 1], src * CORES + c, s).wait_recv()
            when(owns(src), wait)
            start(owns(src), remote(spot, spot, mg_s.at[i, d], mg_r.at[i, d], mate, s))

    def stage_close(i):
        rows = slice(i * row_t, (i + 1) * row_t)
        for d in range(chips):
            src = lax.rem(q + chips - d, chips)

            def wait(src=src, d=d):
                spot = out_ref.at[rows, own_cols(src, 1 - c)]
                remote(spot, spot, mg_s.at[i, d], mg_r.at[i, d], mate, s).wait_recv()
            when(owns(src), wait)

    load_first.wait()
    load_self.wait()
    make_mask(0, 1 - c)
    load_second.wait()
    make_mask(0, c)
    for b in range(blocks):
        for i in range(steps):
            stage_product(b, i)
        for i in range(steps):
            stage_pair(b, i)
        if b == 0:
            for load in load_small:
                load.wait()
            row = lax.broadcasted_iota(jnp.int32, (row_t, row_t), 0)
            col = lax.broadcasted_iota(jnp.int32, (row_t, row_t), 1)
            spread = jnp.where(row == col, jnp.broadcast_to(coup_ref[...], (row_t, row_t)), 0.0)
            weights[...] = jnp.broadcast_to(jnp.sum(spread, axis=1, keepdims=True), weights.shape)

            def first_green():
                green[...] = edge_ref[:, chip_cols(q)].astype(F32)
            when(mine, first_green)
        if b + 1 < blocks:
            make_mask(b + 1, 0)
            make_mask(b + 1, 1)
        for i in range(steps):
            stage_reduce(b, i)
        for i in range(steps):
            if b + 1 < blocks:
                forward_first(b, i)
                forward_rest(b, i)
            else:
                stage_gather(i)
    for i in range(steps):
        stage_close(i)
    for cond, copy in pending:
        when(cond, copy.wait_send)


def local(hist_count, second_count, history, self_rows, edge_rows, step_inv, coupling, reach):
    slab, cols = history.shape
    row_t = step_inv.shape[0]
    steps = self_rows.shape[0] // row_t
    blocks = reach.shape[0]
    chips, planes = hist_count // CORES, second_count
    half = cols // CORES
    owners = min(chips, half // LANES)
    width = half // owners
    assert chips == planes and half == slab
    past, tiles = slab // row_t, cols // row_t
    below = (tiles + 2 + 2 * (blocks - 1)) // (CORES * past)
    slots = planes - 1 + below
    dims = (chips, planes, owners, width, row_t, steps, blocks, below)
    n, m = blocks * steps, (blocks - 1) * steps
    vmem = pl.BlockSpec(memory_space=pltpu.VMEM)
    dma = pltpu.SemaphoreType.DMA
    return pl.pallas_call(
        functools.partial(kernel, dims),
        out_shape=jax.ShapeDtypeStruct((steps * row_t, cols), BF16),
        in_specs=[pl.BlockSpec(memory_space=pl.ANY)] * 5 + [pl.BlockSpec(memory_space=pltpu.SMEM)],
        out_specs=vmem,
        scratch_shapes=[
            pltpu.VMEM((slab, cols), BF16),
            pltpu.VMEM(self_rows.shape, BF16),
            pltpu.VMEM((row_t, half), BF16),
            pltpu.VMEM((row_t, row_t), F32),
            pltpu.VMEM((1, row_t), F32),
            dma((6,)),
            pltpu.VMEM((blocks, slab, cols), BF16),
            pltpu.VMEM((n, row_t, half), BF16),
            pltpu.VMEM((n, row_t, half), BF16),
            pltpu.VMEM((n, row_t, half), BF16),
            pltpu.VMEM((n, row_t, half), BF16),
            pltpu.VMEM((n, chips - 1, row_t, width), BF16),
            pltpu.VMEM((row_t, width), F32),
            pltpu.VMEM((row_t, width), F32),
            pltpu.VMEM((row_t, width), F32),
            pltpu.VMEM((m, row_t, width), BF16),
            pltpu.VMEM((m, slots, row_t, width), BF16),
            pltpu.VMEM((m, row_t, slab), BF16),
            dma((n,)), dma((n,)),
            dma((n, chips - 1)), dma((n, chips - 1)),
            dma((m, slots)), dma((m, slots)),
            dma((m,)), dma((m, slots)), dma((m, chips)),
            dma((steps, chips - 1)), dma((steps, chips - 1)),
            dma((steps, chips)), dma((steps, chips)),
        ],
        compiler_params=pltpu.CompilerParams(
            collective_id=0, has_side_effects=True, vmem_limit_bytes=54 * 1024 * 1024),
        cost_estimate=pl.CostEstimate(
            flops=2 * blocks * steps * row_t * slab * cols, bytes_accessed=2 * slab * cols, transcendentals=0),
    )(history, self_rows, edge_rows, step_inv, coupling.reshape(1, row_t), reach)


def solution(mesh):
    placed = (P("hist", "second"), P(None, "hist"), P(None, "second"), P(), P(), P())
    return jax.shard_map(
        functools.partial(local, mesh.shape["hist"], mesh.shape["second"]),
        mesh=mesh, in_specs=placed, out_specs=P(None, "second"), check_vma=False
    )
```
